32 devices in a mesh: group: 2 (over y), rep: 8 (over z, x), tp: 2 (over core).
Axes of the slice: x: 2, y: 2, z: 4, core: 2. Of those that a mesh axis runs over, the one named last changes fastest.
Arguments:
- queries: bfloat16 [2048, 4096], P(('group', 'rep'), 'tp'), parts along dimension 0, may hold values from -6 to 6
- current_key_value: bfloat16 [2048, 1024], P(('group', 'rep'), 'tp'), parts along dimension 0, may hold values from -6 to 6
- key_value_pool: bfloat16 [1536, 16, 1024], P(('group', 'rep'), None, 'tp'), parts along dimension 0, may hold values from -6 to 6
- request_page_entries: int32 [2048, 4], P(('group', 'rep')), parts along dimension 0, may hold values from 0 to 111, as said below
- context_length: int32 [2048], P(('group', 'rep')), parts along dimension 0, may hold values from 1 to 64, as said below
- migration_page: int32 [96], P(('group', 'rep')), parts along dimension 0, may hold values from 0 to 95, as said below
- migration_target: int32 [96], P(('group', 'rep')), parts along dimension 0, may hold values from 0 to 7, as said below
- adapter_replica: int32 [2048, 1], P(('group', 'rep')), parts along dimension 0, may hold values from 0 to 7; in each aligned block of 128 rows (0 to 127, 128 to 255, ...) at most 32 rows name the same one
- adapter_position: int32 [2048], P(('group', 'rep')), parts along dimension 0, may hold values from 0 to 1
- adapter_down_weight: bfloat16 [16, 4096, 64], P('rep', 'tp'), may hold values from -0.09375 to 0.09375
- adapter_up_weight: bfloat16 [16, 64, 8192], P('rep', None, 'tp'), may hold values from -0.75 to 0.75
Outputs:
- adapter_delta: bfloat16 [2048, 8192], P(('group', 'rep'), 'tp'), parts along dimension 0
The draws below stay inside these ranges and needn't reach their ends.
There are 2 independent parts, one for each index of `group`. The reference program is written for one: setup_inputs(seed, part) draws one part's arguments, and reference() takes and returns one part's arrays. A program takes and returns all parts, laid end to end along the dimension named above; an argument that names none is the same for every part. Nothing has to cross between parts.
Inputs may be any that keep to these rules, and one draw needn't show every extreme that they name: `adapter_replica`: within the 128 rows of one replica no value appears more than 32 times. `migration_target`: A replica's list never names the replica itself and names one destination at most 2 times; every list names some destination exactly 2 times. `migration_page`: the 6 entries of one replica's list are distinct pages of its own pool. `request_page_entries`: an entry of 96 or more names an incoming page that exists for the request's replica. Entries past a request's first ceil(context_length / 16) are 0. `context_length`: every replica holds a request of 64 tokens.
All inputs are finite; a program needn't handle non-finite values.
Results may differ from the reference program's by a relative error of at most 0.009.
Values may be sent and summed in bfloat16 or wider, within the bound.
No kernel may reach another device: no remote copies, remote signals or barrier semaphores. Data moves between devices by JAX's collectives and lax.ppermute only.
A program may use at most 64 MiB of HBM per device.

```python
import math
import jax
import jax.numpy as jnp
import numpy as np
from jax import lax

MODEL_WIDTH = 8192
HEAD_SIZE = 128
KEY_VALUE_HEADS = 4
QUERY_GROUP = 8
ADAPTER_RANK = 64
ADP_DEV = 2
ADAPTER_TOTAL = 16
R_DEV = 128
REQUESTS = 1024
CAP = 32
PAGE = 16
P_DEV = 96
MCAP = 2
MIG = 6
MAXP = 4
N_REP = 8


def layout(key):
    streams = jax.random.split(jax.random.fold_in(key, 101), 8)
    forced = 1 + jax.random.randint(streams[0], (N_REP,), 0, N_REP - 1)
    labels = jax.vmap(lambda stream: jax.random.permutation(stream, (N_REP - 2) * MCAP))(jax.random.split(streams[1], N_REP))
    offsets = 1 + labels[:, :MIG - MCAP] // MCAP
    offsets = jnp.where(offsets >= forced[:, None], offsets + 1, offsets)
    offsets = jnp.concatenate([jnp.broadcast_to(forced[:, None], (N_REP, MCAP)), offsets], axis=1).astype(jnp.int32)
    shuffle = jax.vmap(lambda stream: jax.random.permutation(stream, MIG))(jax.random.split(streams[2], N_REP))
    offsets = jnp.take_along_axis(offsets, shuffle, axis=1)
    targets = ((jnp.arange(N_REP, dtype=jnp.int32)[:, None] + offsets) % N_REP).astype(jnp.int32)
    chosen = jax.vmap(lambda stream: jax.random.permutation(stream, P_DEV)[:MIG])(jax.random.split(streams[3], N_REP))
    received = jnp.sum((targets[:, :, None] == jnp.arange(N_REP, dtype=jnp.int32)[None, None, :]).astype(jnp.int32), axis=1)
    live_slots = (jnp.arange(MCAP, dtype=jnp.int32)[None, None, :] < received.T[:, :, None]).reshape(N_REP, N_REP * MCAP).astype(jnp.int32)
    live_count = jnp.sum(live_slots, axis=1)
    running = jnp.cumsum(live_slots, axis=1)
    coin_flips = jax.random.randint(streams[4], (N_REP, R_DEV * MAXP), 0, 2)
    pick_index = jax.random.randint(streams[5], (N_REP, R_DEV * MAXP), 0, 1 << 20) % jnp.maximum(live_count, 1)[:, None]
    slot_ids = jax.vmap(lambda running_row, wanted: jnp.searchsorted(running_row, wanted, side='right'))(running, pick_index).astype(jnp.int32)
    local_pages = jax.random.randint(streams[6], (N_REP, R_DEV * MAXP), 0, P_DEV)
    use_in = (coin_flips == 1) & (live_count[:, None] > 0)
    entries = jnp.where(use_in, P_DEV + slot_ids, local_pages).reshape(N_REP, R_DEV, MAXP)
    lengths = jax.random.randint(streams[7], (N_REP, R_DEV), 1, MAXP * PAGE + 1)
    longest = jax.random.randint(jax.random.fold_in(streams[7], 1), (N_REP,), 0, R_DEV)
    lengths = jnp.where(jnp.arange(R_DEV, dtype=jnp.int32)[None, :] == longest[:, None], MAXP * PAGE, lengths)
    needed = (lengths + PAGE - 1) // PAGE
    entries = jnp.where(jnp.arange(MAXP, dtype=jnp.int32)[None, None, :] < needed[:, :, None], entries, 0)
    return (chosen.reshape(-1).astype(jnp.int32), targets.reshape(-1), entries.reshape(N_REP * R_DEV, MAXP).astype(jnp.int32), lengths.reshape(-1).astype(jnp.int32))


def draw_migration_page(key, part):
    return layout(key)[0]


def draw_migration_target(key, part):
    return layout(key)[1]


def draw_request_page_entries(key, part):
    return layout(key)[2]


def draw_context_length(key, part):
    return layout(key)[3]


def draw_key_value_pool(key, part):
    key = jax.random.fold_in(key, 7)
    first_key = jax.random.fold_in(key, 0)
    pool_shape = (N_REP * P_DEV, PAGE, KEY_VALUE_HEADS, 2, HEAD_SIZE)
    page_pool = jnp.clip(jax.random.normal(first_key, pool_shape, jnp.float32), -6.0, 6.0)
    return page_pool.reshape(N_REP * P_DEV, PAGE, KEY_VALUE_HEADS * 2 * HEAD_SIZE).astype(jnp.bfloat16)


def draw_queries(key, part):
    key = jax.random.fold_in(key, 5)
    first_key = jax.random.fold_in(key, 0)
    query_shape = (REQUESTS, KEY_VALUE_HEADS * QUERY_GROUP * HEAD_SIZE)
    result = jnp.clip(jax.random.normal(first_key, query_shape, jnp.float32), -6.0, 6.0)
    return result.astype(jnp.bfloat16)


def touch_ends(drawn, rng, least, largest):
    longest = drawn.shape.index(max(drawn.shape))
    spots = []
    for shift in (0, 1):
        where = [jax.random.randint(jax.random.fold_in(rng, axis), (), 0, length) for axis, length in enumerate(drawn.shape)]
        where[longest] = (where[longest] + shift) % drawn.shape[longest]
        spots.append(tuple(where))
    return drawn.at[spots[0]].set(least).at[spots[1]].set(largest)


def steps_of(own_key, shape, cuts, low, top_value):
    loudness, own = 1.0, jax.random.fold_in(own_key, 6)
    for dim, blocks in cuts:
        draws = jnp.exp(jax.random.uniform(jax.random.fold_in(own, dim), (blocks,), jnp.float32, low / len(cuts), top_value / len(cuts)))
        loudness = loudness * jnp.repeat(draws, shape[dim] // blocks).reshape([-1 if axis == dim else 1 for axis in range(len(shape))])
    return loudness


def routed_block(rng, own, number, rows, amount, top, reach, slope):
    ranking = jax.random.permutation(rng, amount)
    crowded, usual = load_shares(amount, rows * top, reach, slope, True), load_shares(amount, rows * top, reach, slope, False)
    places = jnp.arange(amount)

    def named(tallies, offset_by):
        used = int((tallies > 0).sum())
        fixed = max(1, used // 4)
        passed = fixed + (places - fixed + offset_by * (used - fixed)) % max(1, amount - fixed)
        return jnp.zeros((amount,), jnp.int32).at[ranking[jnp.where(places < fixed, places, passed)]].set(jnp.asarray(tallies, jnp.int32))

    tallies = jnp.where(number % 4 == 0, named(crowded, number // 4), named(usual, number - number // 4 - 1))
    mixed = jax.random.permutation(jax.random.fold_in(own, 3), amount)
    donor, receiver = mixed[0:amount // 2 * 2:2], mixed[1:amount // 2 * 2:2]
    room = jnp.minimum(tallies[donor] - 1, reach - tallies[receiver]) // 2
    room = jnp.where((donor == ranking[0]) | (receiver == ranking[0]) | (tallies[receiver] == 0), 0, jnp.maximum(room, 0))
    passed = jax.random.randint(jax.random.fold_in(own, 4), (amount // 2,), 0, 1 << 20) % (room + 1)
    tallies = tallies.at[donor].add(-passed).at[receiver].add(passed)
    items = jnp.searchsorted(jnp.cumsum(tallies), jnp.arange(rows * top), side="right").astype(jnp.int32)
    table = items.reshape(top, rows).T
    table = table[jax.random.permutation(jax.random.fold_in(own, 1), rows)]
    offset_by = jax.random.randint(jax.random.fold_in(own, 2), (rows, 1), 0, top)
    return jnp.take_along_axis(table, (jnp.arange(top)[None, :] + offset_by) % top, axis=1)


def load_shares(amount, total, reach, skew, full):
    weights = [(1 << 20) // math.isqrt(grade ** skew) + 1 for grade in range(1, amount + 1)]
    largest = reach if full else min(reach, max(-(-total // amount), total * weights[0] // sum(weights)))
    least = 1 if total - largest >= amount - 1 else 0
    counts, surplus = [largest] + [least] * (amount - 1), total - largest - least * (amount - 1)
    while surplus > 0:
        free = [i for i in range(1, amount) if counts[i] < largest] or [i for i in range(1, amount) if counts[i] < reach]
        mass, remaining = sum([weights[i] for i in free]), surplus
        for i in free:
            extra = min(reach - counts[i], max(1, remaining * weights[i] // mass), surplus)
            counts[i] = counts[i] + extra
            surplus = surplus - extra
    return np.array(counts)


def noise(own_key, dims, deviation, reach, cuts=(), kind=jnp.bfloat16):
    values = deviation * jax.random.normal(own_key, dims, jnp.float32)
    if cuts:
        values = values * steps_of(own_key, dims, cuts, -0.22, 0.18)
    return jnp.clip(values, -reach, reach).astype(kind)


def setup_inputs(seed: int = 0, part: int = 0) -> dict:
    key_of = jax.random.split(jax.random.key(seed), 12)
    part_splits = jax.random.split(jax.random.fold_in(key_of[11], part), 12)
    queries = draw_queries(jax.random.fold_in(jax.random.fold_in(key_of[11], part), 71), part)
    current_key_value = noise(part_splits[1], (REQUESTS, KEY_VALUE_HEADS * 2 * HEAD_SIZE), 1.0, 6.0, ((0, 8), (1, 2)))
    key_value_pool = draw_key_value_pool(jax.random.fold_in(jax.random.fold_in(key_of[11], part), 71), part)
    request_page_entries = draw_request_page_entries(jax.random.fold_in(jax.random.fold_in(key_of[11], part), 71), part)
    context_length = draw_context_length(jax.random.fold_in(jax.random.fold_in(key_of[11], part), 71), part)
    migration_page = draw_migration_page(jax.random.fold_in(jax.random.fold_in(key_of[11], part), 71), part)
    migration_target = draw_migration_target(jax.random.fold_in(jax.random.fold_in(key_of[11], part), 71), part)
    adapter_replica_keys = jax.random.split(jax.random.fold_in(part_splits[7], 1), REQUESTS // R_DEV)
    adapter_replica_turns = jax.random.permutation(jax.random.fold_in(part_splits[7], 3), REQUESTS // R_DEV)
    adapter_replica = jax.vmap(lambda own, number: routed_block(jax.random.fold_in(part_splits[7], 2), own, number, R_DEV, N_REP, 1, CAP, 2))(adapter_replica_keys, adapter_replica_turns).reshape((REQUESTS, 1))
    adapter_position = touch_ends(jax.random.randint(part_splits[8], (REQUESTS,), 0, ADP_DEV), jax.random.fold_in(part_splits[8], 1), 0, ADP_DEV - 1).astype(jnp.int32)
    adapter_down_weight = noise(key_of[9], (ADAPTER_TOTAL, KEY_VALUE_HEADS * QUERY_GROUP * HEAD_SIZE, ADAPTER_RANK), (KEY_VALUE_HEADS * QUERY_GROUP * HEAD_SIZE) ** -0.5, 0.09375, ((0, 8), (1, 2)))
    adapter_up_weight = noise(key_of[10], (ADAPTER_TOTAL, ADAPTER_RANK, MODEL_WIDTH), ADAPTER_RANK ** -0.5, 0.75, ((0, 8), (2, 2)))
    return {"queries": queries, "current_key_value": current_key_value, "key_value_pool": key_value_pool, "request_page_entries": request_page_entries, "context_length": context_length, "migration_page": migration_page, "migration_target": migration_target, "adapter_replica": adapter_replica, "adapter_position": adapter_position, "adapter_down_weight": adapter_down_weight, "adapter_up_weight": adapter_up_weight}


def rounded(values):
    return lax.optimization_barrier(values.astype(jnp.bfloat16))

def reference(queries, current_key_value, key_value_pool, request_page_entries, context_length, migration_page, migration_target, adapter_replica, adapter_position, adapter_down_weight, adapter_up_weight):
    targets = migration_target.reshape(N_REP, MIG)
    sources = migration_page.reshape(N_REP, MIG)
    position = jnp.arange(MIG, dtype=jnp.int32)
    earlier = position[None, :] < position[:, None]
    before_count = lax.optimization_barrier(jnp.sum(((targets[:, :, None] == targets[:, None, :]) & earlier[None]).astype(jnp.int32), axis=2))
    page_pool = key_value_pool.reshape(N_REP, P_DEV, PAGE, KEY_VALUE_HEADS * 2 * HEAD_SIZE)
    score_scale = 1.0 / math.sqrt(HEAD_SIZE)

    def one_replica(replica):
        start = replica * R_DEV
        table = lax.dynamic_slice_in_dim(request_page_entries, start, R_DEV, 0)
        lengths = lax.dynamic_slice_in_dim(context_length, start, R_DEV, 0)
        incoming = table >= P_DEV
        code = jnp.maximum(table - P_DEV, 0)
        anchor = (code // MCAP).astype(jnp.int32)
        within = (code % MCAP).astype(jnp.int32)
        match = (targets[anchor] == replica) & (before_count[anchor] == within[:, :, None])
        entry = lax.optimization_barrier(jnp.sum(jnp.where(match, position, 0), axis=2)).astype(jnp.int32)
        remote = sources[anchor, entry]
        owner = jnp.where(incoming, anchor, replica).astype(jnp.int32)
        page_ids = jnp.where(incoming, remote, table).astype(jnp.int32)
        blocks = page_pool[owner, page_ids].reshape(R_DEV, MAXP * PAGE, KEY_VALUE_HEADS, 2, HEAD_SIZE).astype(jnp.float32)
        key_rows = blocks[:, :, :, 0, :]
        value_rows = blocks[:, :, :, 1, :]
        query_heads = lax.dynamic_slice_in_dim(queries, start, R_DEV, 0).astype(jnp.float32).reshape(R_DEV, KEY_VALUE_HEADS, QUERY_GROUP, HEAD_SIZE)
        fresh = lax.dynamic_slice_in_dim(current_key_value, start, R_DEV, 0).astype(jnp.float32).reshape(R_DEV, KEY_VALUE_HEADS, 2, HEAD_SIZE)
        scores = jnp.einsum('rgjk,rtgk->rgjt', query_heads, key_rows) * score_scale
        visible = jnp.arange(MAXP * PAGE, dtype=jnp.int32)[None, :] < lengths[:, None]
        scores = jnp.where(visible[:, None, None, :], scores, -1e+30)
        own_score = jnp.einsum('rgjk,rgk->rgj', query_heads, fresh[:, :, 0, :]) * score_scale
        row_max = jnp.maximum(lax.optimization_barrier(jnp.max(scores, axis=3)), own_score)
        weights = jnp.exp(scores - row_max[:, :, :, None])
        own_weight = jnp.exp(own_score - row_max)
        normaliser = lax.optimization_barrier(jnp.sum(weights, axis=3)) + own_weight
        probabilities = rounded(weights / normaliser[:, :, :, None]).astype(jnp.float32)
        own_prob = rounded(own_weight / normaliser).astype(jnp.float32)
        attended = jnp.einsum('rgjt,rtgk->rgjk', probabilities, value_rows)
        attended = attended + own_prob[:, :, :, None] * fresh[:, :, None, 1, :]
        heads_out = rounded(attended.reshape(R_DEV, KEY_VALUE_HEADS * QUERY_GROUP * HEAD_SIZE))
        home_ids = lax.dynamic_slice_in_dim(adapter_replica[:, 0], start, R_DEV, 0)
        slot_ids = lax.dynamic_slice_in_dim(adapter_position, start, R_DEV, 0)
        adapter_index = (home_ids * ADP_DEV + slot_ids).astype(jnp.int32)
        down_matrix_rows = adapter_down_weight[adapter_index].astype(jnp.float32)
        low_rank = rounded(jnp.einsum('rk,rkq->rq', heads_out.astype(jnp.float32), down_matrix_rows))
        up_matrix_rows = adapter_up_weight[adapter_index].astype(jnp.float32)
        return jnp.einsum('rq,rqd->rd', low_rank.astype(jnp.float32), up_matrix_rows).astype(jnp.bfloat16)
    delta = lax.map(one_replica, jnp.arange(N_REP, dtype=jnp.int32))
    return delta.reshape(REQUESTS, MODEL_WIDTH)
```

```python
import functools
import math

import jax
import jax.numpy as jnp
from jax import lax
from jax.experimental import pallas as pl
from jax.experimental.pallas import tpu as pltpu
from jax.sharding import PartitionSpec as P

HEAD_SIZE = 128
QUERY_GROUP = 8
MCAP = 2
LANES = 128
TOKEN_STEP = 256
HIDDEN = -1e30
SCORE_SCALE = math.log2(math.e) / math.sqrt(HEAD_SIZE)
VMEM_LIMIT = 48 * 1024 * 1024


def vmem_spec():
    return pl.BlockSpec(memory_space=pltpu.VMEM)


def smem_spec():
    return pl.BlockSpec(memory_space=pltpu.SMEM)


def params():
    return pltpu.CompilerParams(vmem_limit_bytes=VMEM_LIMIT)


def row_to_column(row):
    count = row.shape[1]
    across = lax.broadcasted_iota(jnp.int32, (count, count), 1)
    down = lax.broadcasted_iota(jnp.int32, (count, count), 0)
    return jnp.sum(jnp.where(across == down, row, 0), axis=1, keepdims=True)


def column_to_row(column):
    count = column.shape[0]
    across = lax.broadcasted_iota(jnp.int32, (count, count), 1)
    down = lax.broadcasted_iota(jnp.int32, (count, count), 0)
    return jnp.sum(jnp.where(across == down, column, 0), axis=0, keepdims=True)


def outgoing_kernel(page_ref, target_ref, pool_ref, out_ref, count_ref, chosen_ref):
    entry_number = page_ref.shape[0]
    slot_number = out_ref.shape[0]

    def clear(slot, carry):
        chosen_ref[slot] = 0
        count_ref[slot // MCAP] = 0
        return carry

    def place(entry, carry):
        target = target_ref[entry]
        rank = count_ref[target]
        chosen_ref[target * MCAP + rank] = page_ref[entry]
        count_ref[target] = rank + 1
        return carry

    def copy(slot, carry):
        out_ref[slot] = pool_ref[chosen_ref[slot]]
        return carry

    lax.fori_loop(0, slot_number, clear, 0)
    lax.fori_loop(0, entry_number, place, 0)
    lax.fori_loop(0, slot_number, copy, 0)


def outgoing_pages(migration_page, migration_target, pool, replicas):
    slots = replicas * MCAP
    return pl.pallas_call(
        outgoing_kernel,
        out_shape=jax.ShapeDtypeStruct((slots,) + pool.shape[1:], pool.dtype),
        in_specs=[smem_spec(), smem_spec(), vmem_spec()],
        out_specs=vmem_spec(),
        scratch_shapes=[pltpu.SMEM((replicas,), jnp.int32), pltpu.SMEM((slots,), jnp.int32)],
        compiler_params=params(),
        name="outgoing_pages",
    )(migration_page, migration_target, pool)


def token_bias(entries, lengths, first_token, tokens, page_len):
    rows = entries.shape[0]
    token = first_token + lax.broadcasted_iota(jnp.int32, (rows, tokens), 1)
    seen = jnp.zeros((rows, tokens), jnp.float32)
    for e in range(entries.shape[1]):
        low = entries[:, e : e + 1] * page_len
        high = low + jnp.clip(lengths - e * page_len, 0, page_len)
        seen = seen + jnp.where((token >= low) & (token < high), 1.0, 0.0)
    return jnp.where(seen > 0.0, jnp.log2(jnp.maximum(seen, 1.0)), HIDDEN)


def fill_bias(bias_ref, entries_ref, length_ref, first_token, page_len):
    lengths = row_to_column(length_ref[...])
    entries = entries_ref[...]
    for start in range(0, bias_ref.shape[1], TOKEN_STEP):
        size = min(TOKEN_STEP, bias_ref.shape[1] - start)
        bias_ref[:, start : start + size] = token_bias(
            entries, lengths, first_token + start, size, page_len
        )


def lane_folds(values, combine):
    folded = values[:, :LANES]
    for start in range(LANES, values.shape[1], LANES):
        folded = combine(folded, values[:, start : start + LANES])
    return folded


def score_tokens(stacked, keys, bias_ref, score_ref, top_ref):
    rows = bias_ref.shape[0]
    tokens = bias_ref.shape[1]
    for start in range(0, tokens, TOKEN_STEP):
        size = min(TOKEN_STEP, tokens - start)
        part = lax.dot_general(
            stacked,
            keys(start, size),
            (((1,), (1,)), ((), ())),
            preferred_element_type=jnp.float32,
        )
        bias = bias_ref[:, start : start + size]
        for h in range(QUERY_GROUP):
            own = slice(h * rows, (h + 1) * rows)
            shifted = part[own] * SCORE_SCALE + bias
            score_ref[own, start : start + size] = shifted
            top = lane_folds(shifted, jnp.maximum)
            top_ref[own, :] = top if start == 0 else jnp.maximum(top_ref[own, :], top)


def weigh_tokens(own, top, score_ref, weight_ref):
    tokens = score_ref.shape[1]
    total = None
    for start in range(0, tokens, TOKEN_STEP):
        size = min(TOKEN_STEP, tokens - start)
        weights = jnp.exp2(score_ref[own, start : start + size] - top)
        weight_ref[own, start : start + size] = weights.astype(jnp.bfloat16)
        folded = lane_folds(weights, jnp.add)
        total = folded if total is None else total + folded
    return jnp.sum(total, axis=1, keepdims=True)


def stack_heads(query_ref, stacked_ref, first_head):
    rows = query_ref.shape[0]
    for h in range(QUERY_GROUP):
        place = (first_head + h) * HEAD_SIZE
        stacked_ref[h * rows : (h + 1) * rows, :] = query_ref[:, place : place + HEAD_SIZE]


def pool_kernel(
    page_len,
    query_ref,
    pool_ref,
    entries_ref,
    length_ref,
    part_ref,
    stat_ref,
    bias_ref,
    stacked_ref,
    score_ref,
    weight_ref,
    top_ref,
):
    @pl.when(pl.program_id(0) == 0)
    def _():
        fill_bias(bias_ref, entries_ref, length_ref, 0, page_len)

    rows = query_ref.shape[0]
    stack_heads(query_ref, stacked_ref, 0)
    score_tokens(
        stacked_ref[...],
        lambda start, size: pool_ref[start : start + size, :HEAD_SIZE],
        bias_ref,
        score_ref,
        top_ref,
    )
    lane = lax.broadcasted_iota(jnp.int32, (rows, LANES), 1)
    stats = jnp.zeros((rows, LANES), jnp.float32)
    for h in range(QUERY_GROUP):
        own = slice(h * rows, (h + 1) * rows)
        top = jnp.max(top_ref[own, :], axis=1, keepdims=True)
        total = weigh_tokens(own, top, score_ref, weight_ref)
        stats = jnp.where(lane == h, top, stats)
        stats = jnp.where(lane == QUERY_GROUP + h, total, stats)
    stat_ref[...] = stats
    parts = jnp.dot(
        weight_ref[...], pool_ref[:, HEAD_SIZE:], preferred_element_type=jnp.float32
    )
    for h in range(QUERY_GROUP):
        part_ref[:, h * HEAD_SIZE : (h + 1) * HEAD_SIZE] = parts[h * rows : (h + 1) * rows]


def attend_pool(queries, pool, entries, lengths, page_len):
    rows = queries.shape[0]
    tokens = pool.shape[0]
    kv_local = pool.shape[1] // (2 * HEAD_SIZE)
    wide = QUERY_GROUP * HEAD_SIZE
    stacked = QUERY_GROUP * rows
    return pl.pallas_call(
        functools.partial(pool_kernel, page_len),
        grid=(kv_local,),
        out_shape=(
            jax.ShapeDtypeStruct((rows, kv_local * wide), jnp.float32),
            jax.ShapeDtypeStruct((rows, kv_local * LANES), jnp.float32),
        ),
        in_specs=[
            pl.BlockSpec((rows, wide), lambda g: (0, g)),
            pl.BlockSpec((tokens, 2 * HEAD_SIZE), lambda g: (0, g)),
            pl.BlockSpec(entries.shape, lambda g: (0, 0)),
            pl.BlockSpec(lengths.shape, lambda g: (0, 0)),
        ],
        out_specs=(
            pl.BlockSpec((rows, wide), lambda g: (0, g)),
            pl.BlockSpec((rows, LANES), lambda g: (0, g)),
        ),
        scratch_shapes=[
            pltpu.VMEM((rows, tokens), jnp.float32),
            pltpu.VMEM((stacked, HEAD_SIZE), jnp.bfloat16),
            pltpu.VMEM((stacked, tokens), jnp.float32),
            pltpu.VMEM((stacked, tokens), jnp.bfloat16),
            pltpu.VMEM((stacked, LANES), jnp.float32),
        ],
        compiler_params=params(),
        cost_estimate=pl.CostEstimate(
            flops=4 * kv_local * stacked * tokens * HEAD_SIZE,
            bytes_accessed=2 * (queries.size + pool.size) + 4 * queries.size,
            transcendentals=kv_local * stacked * tokens,
        ),
        name="attend_pool",
    )(queries, pool, entries, lengths)


def finish_kernel(
    page_len,
    first_token,
    query_ref,
    arrived_ref,
    fresh_ref,
    entries_ref,
    length_ref,
    part_ref,
    stat_ref,
    slot_ref,
    position_ref,
    *refs,
):
    out_refs, (bias_ref, stacked_ref, score_ref, weight_ref, top_ref, heads_ref) = refs[:-6], refs[-6:]
    rows = query_ref.shape[0]
    kv_local = arrived_ref.shape[1] // (2 * HEAD_SIZE)
    wide = QUERY_GROUP * HEAD_SIZE
    fill_bias(bias_ref, entries_ref, length_ref, first_token, page_len)
    for g in range(kv_local):
        place = g * 2 * HEAD_SIZE
        stack_heads(query_ref, stacked_ref, g * QUERY_GROUP)
        score_tokens(
            stacked_ref[...],
            lambda start, size: arrived_ref[start : start + size, place : place + HEAD_SIZE],
            bias_ref,
            score_ref,
            top_ref,
        )
        new_key = fresh_ref[:, place : place + HEAD_SIZE].astype(jnp.float32)
        new_value = fresh_ref[:, place + HEAD_SIZE : place + 2 * HEAD_SIZE].astype(jnp.float32)
        scale_old, own_weight, total = [], [], []
        for h in range(QUERY_GROUP):
            own = slice(h * rows, (h + 1) * rows)
            query = stacked_ref[own, :].astype(jnp.float32)
            own_score = jnp.sum(query * new_key, axis=1, keepdims=True) * SCORE_SCALE
            old_top = stat_ref[:, g * LANES + h : g * LANES + h + 1]
            old_total = stat_ref[:, g * LANES + QUERY_GROUP + h : g * LANES + QUERY_GROUP + h + 1]
            top = jnp.max(top_ref[own, :], axis=1, keepdims=True)
            top = jnp.maximum(jnp.maximum(top, own_score), old_top)
            scale_old.append(jnp.exp2(old_top - top))
            own_weight.append(jnp.exp2(own_score - top))
            fresh_total = weigh_tokens(own, top, score_ref, weight_ref)
            total.append(scale_old[h] * old_total + fresh_total + own_weight[h])
        parts = jnp.dot(
            weight_ref[...],
            arrived_ref[:, place + HEAD_SIZE : place + 2 * HEAD_SIZE],
            preferred_element_type=jnp.float32,
        )
        for h in range(QUERY_GROUP):
            column = g * wide + h * HEAD_SIZE
            heads = parts[h * rows : (h + 1) * rows] + own_weight[h] * new_value
            heads = heads + scale_old[h] * part_ref[:, column : column + HEAD_SIZE]
            heads_ref[:, column : column + HEAD_SIZE] = (heads / total[h]).astype(jnp.bfloat16)
    width = query_ref.shape[1]
    first = 0
    for out_ref in out_refs:
        slots = out_ref.shape[0]
        slot = first + lax.broadcasted_iota(jnp.int32, (slots, rows), 0)
        pick = slot == slot_ref[...]
        label = jnp.sum(jnp.where(pick, position_ref[...], 0), axis=1, keepdims=True)
        pick = pick.astype(jnp.float32).astype(jnp.bfloat16)
        for start in range(0, width, wide):
            out_ref[:, start : start + wide] = jnp.dot(
                pick, heads_ref[:, start : start + wide], preferred_element_type=jnp.float32
            ).astype(jnp.bfloat16)
        out_ref[:, width:] = jnp.broadcast_to(
            label.astype(jnp.float32).astype(jnp.bfloat16), (slots, LANES)
        )
        first += slots


def finish_attention(
    queries, arrived, fresh, entries, lengths, parts, stats, slots, positions, page_len, first_token, blocks
):
    rows, width = queries.shape
    tokens = arrived.shape[0]
    stacked = QUERY_GROUP * rows
    return pl.pallas_call(
        functools.partial(finish_kernel, page_len, first_token),
        out_shape=tuple(
            jax.ShapeDtypeStruct((block, width + LANES), jnp.bfloat16) for block in blocks
        ),
        in_specs=[vmem_spec()] * 9,
        out_specs=tuple(vmem_spec() for _ in blocks),
        scratch_shapes=[
            pltpu.VMEM((rows, tokens), jnp.float32),
            pltpu.VMEM((stacked, HEAD_SIZE), jnp.bfloat16),
            pltpu.VMEM((stacked, tokens), jnp.float32),
            pltpu.VMEM((stacked, tokens), jnp.bfloat16),
            pltpu.VMEM((stacked, LANES), jnp.float32),
            pltpu.VMEM((rows, width), jnp.bfloat16),
        ],
        compiler_params=params(),
        cost_estimate=pl.CostEstimate(
            flops=4 * tokens * rows * width,
            bytes_accessed=12 * rows * width,
            transcendentals=tokens * rows * width // HEAD_SIZE,
        ),
        name="finish_attention",
    )(queries, arrived, fresh, entries, lengths, parts, stats, slots, positions)


def rank_among(targets):
    position = jnp.arange(targets.shape[0], dtype=jnp.int32)
    same = (targets[:, None] == targets[None, :]) & (position[:, None] < position[None, :])
    return jnp.sum(same.astype(jnp.int32), axis=0)


def attention(
    queries,
    current_key_value,
    key_value_pool,
    request_page_entries,
    context_length,
    migration_page,
    migration_target,
    slots,
    adapter_position,
    blocks,
):
    replicas = lax.axis_size("rep")
    pages, page_len, features = key_value_pool.shape
    lengths = context_length.reshape(1, -1)
    outgoing = outgoing_pages(migration_page, migration_target, key_value_pool, replicas)
    arrived = lax.all_to_all(outgoing, "rep", split_axis=0, concat_axis=0, tiled=True)
    parts, stats = attend_pool(
        queries,
        key_value_pool.reshape(pages * page_len, features),
        request_page_entries,
        lengths,
        page_len,
    )
    return finish_attention(
        queries,
        arrived.reshape(-1, features),
        current_key_value,
        request_page_entries,
        lengths,
        parts,
        stats,
        slots,
        adapter_position.reshape(1, -1),
        page_len,
        pages * page_len,
        blocks,
    )


def local(
    queries,
    current_key_value,
    key_value_pool,
    request_page_entries,
    context_length,
    migration_page,
    migration_target,
    adapter_replica,
    adapter_position,
    adapter_down_weight,
    adapter_up_weight,
):
    replicas = lax.axis_size("rep")
    rows, width = queries.shape
    adapter_number = adapter_down_weight.shape[0]
    slot_cap = max(2, (2 * rows + replicas - 1) // replicas)
    targets = adapter_replica[:, 0]
    slot_index = targets * slot_cap + rank_among(targets)
    (outbound,) = attention(
        queries,
        current_key_value,
        key_value_pool,
        request_page_entries,
        context_length,
        migration_page,
        migration_target,
        slot_index.reshape(1, -1),
        adapter_position,
        (replicas * slot_cap,),
    )
    outbound = outbound.reshape(replicas, slot_cap, -1)
    activations = lax.all_to_all(outbound, "rep", split_axis=0, concat_axis=0, tiled=True)
    shape_in = activations.shape
    flat_output = activations.reshape(-1, shape_in[2])
    selector = (
        flat_output[:, width : width + 1].astype(jnp.int32)
        == jnp.arange(adapter_number, dtype=jnp.int32)[None, :]
    )
    reduced_rank_total = jnp.einsum(
        "oh,pht->opt", flat_output[:, :width], adapter_down_weight, preferred_element_type=jnp.float32
    )
    partial_low = jnp.sum(jnp.where(selector[:, :, None], reduced_rank_total, 0.0), axis=1)
    low_rank = lax.psum(partial_low, "tp").astype(jnp.bfloat16)
    broadcast_result = jnp.where(
        selector[:, :, None], low_rank[:, None, :], jnp.zeros((), jnp.bfloat16)
    )
    broadcast_result = broadcast_result.reshape(flat_output.shape[0], -1)
    lifted = jnp.dot(
        broadcast_result,
        adapter_up_weight.reshape(-1, adapter_up_weight.shape[2]),
        preferred_element_type=jnp.float32,
    )
    lifted = lifted.astype(jnp.bfloat16).reshape(shape_in[0], shape_in[1], -1)
    returned = lax.all_to_all(lifted, "rep", split_axis=0, concat_axis=0, tiled=True)
    route_mask = (
        jnp.arange(replicas * slot_cap, dtype=jnp.int32)[:, None] == slot_index[None, :]
    ).astype(jnp.bfloat16)
    delta = jnp.einsum(
        "sr,sd->rd",
        route_mask,
        returned.reshape(replicas * slot_cap, -1),
        preferred_element_type=jnp.float32,
    )
    return delta.astype(jnp.bfloat16)


def solution(mesh):
    return jax.shard_map(
        local,
        mesh=mesh,
        in_specs=(
            P(("group", "rep"), "tp"),
            P(("group", "rep"), "tp"),
            P(("group", "rep"), None, "tp"),
            P(("group", "rep"), None),
            P(("group", "rep")),
            P(("group", "rep")),
            P(("group", "rep")),
            P(("group", "rep"), None),
            P(("group", "rep")),
            P("rep", "tp", None),
            P("rep", None, "tp"),
        ),
        out_specs=P(("group", "rep"), "tp"),
        check_vma=False,
    )
```

```python
import functools
import math

import jax
import jax.numpy as jnp
from jax import lax
from jax.experimental import pallas as pl
from jax.experimental.pallas import tpu as pltpu
from jax.sharding import PartitionSpec as P

HEAD_SIZE = 128
QUERY_GROUP = 8
MCAP = 2
LANES = 128
TOKEN_STEP = 256
HIDDEN = -1e30
SCORE_SCALE = math.log2(math.e) / math.sqrt(HEAD_SIZE)
BIAS_UNIT = float(jnp.bfloat16(1.0 / SCORE_SCALE))
HEADS_STEP = 2
MIB = 1024 * 1024


def whole(array):
    shape = array.shape
    return pl.BlockSpec(shape, lambda *step: (0,) * len(shape))


def smem_spec():
    return pl.BlockSpec(memory_space=pltpu.SMEM)


def params(mebibytes=24):
    return pltpu.CompilerParams(vmem_limit_bytes=mebibytes * MIB)


def cost():
    return pl.CostEstimate(flops=1024, bytes_accessed=1024, transcendentals=0)


def row_to_column(row):
    count = row.shape[1]
    across = lax.broadcasted_iota(jnp.int32, (count, count), 1)
    down = lax.broadcasted_iota(jnp.int32, (count, count), 0)
    return jnp.sum(jnp.where(across == down, row, 0), axis=1, keepdims=True)


def outgoing_kernel(pieces, half_ref, page_ref, target_ref, pool_ref, *refs):
    count_ref, chosen_ref, page_sem, share_sem = refs[-4:]
    out_ref, share_refs, mine_refs = refs[len(pieces)], refs[: len(pieces)], refs[len(pieces) + 1 : -4]
    entry_number = page_ref.shape[0]
    slot_number = out_ref.shape[0]

    def clear(slot, carry):
        chosen_ref[slot] = 0
        count_ref[slot // MCAP] = 0
        return carry

    def place(entry, carry):
        target = target_ref[entry]
        rank = count_ref[target]
        chosen_ref[target * MCAP + rank] = page_ref[entry]
        count_ref[target] = rank + 1
        return carry

    def page_copy(slot):
        return pltpu.make_async_copy(
            pool_ref.at[chosen_ref[slot]], out_ref.at[slot], page_sem.at[slot]
        )

    def send(slot, carry):
        page_copy(slot).start()
        return carry

    def finish(slot, carry):
        page_copy(slot).wait()
        return carry

    shares = []
    for share, cuts in zip(share_refs, pieces):
        for first, last, pack, start in cuts:
            shares.append(
                pltpu.make_async_copy(
                    share.at[half_ref[0], :, pl.ds(first, last - first)],
                    mine_refs[pack].at[:, pl.ds(start, last - first)],
                    share_sem.at[len(shares)],
                )
            )
    lax.fori_loop(0, slot_number, clear, 0)
    lax.fori_loop(0, entry_number, place, 0)
    lax.fori_loop(0, slot_number, send, 0)
    for share in shares:
        share.start()
    lax.fori_loop(0, slot_number, finish, 0)
    for share in shares:
        share.wait()


def outgoing_pages(half, migration_page, migration_target, pool, replicas, shares=(), pieces=(), packs=()):
    slots = replicas * MCAP
    hbm = pl.BlockSpec(memory_space=pltpu.HBM)
    out_shape = [jax.ShapeDtypeStruct((slots,) + pool.shape[1:], pool.dtype)]
    out_shape += [jax.ShapeDtypeStruct(pack, pool.dtype) for pack in packs]
    return pl.pallas_call(
        functools.partial(outgoing_kernel, pieces),
        out_shape=out_shape,
        in_specs=[smem_spec()] * 3 + [hbm] * (1 + len(shares)),
        out_specs=[whole(out) for out in out_shape],
        scratch_shapes=[
            pltpu.SMEM((replicas,), jnp.int32),
            pltpu.SMEM((slots,), jnp.int32),
            pltpu.SemaphoreType.DMA((slots,)),
            pltpu.SemaphoreType.DMA((max(1, sum(len(cuts) for cuts in pieces)),)),
        ],
        compiler_params=params(60),
        cost_estimate=cost(),
        name="outgoing_pages",
    )(half, migration_page, migration_target, pool, *shares)


def token_bias(entries, lengths, first_token, tokens, page_len):
    shape = (tokens, entries.shape[1])
    token = first_token + lax.broadcasted_iota(jnp.int32, shape, 0)
    seen = jnp.zeros(shape, jnp.float32)
    for e in range(entries.shape[0]):
        low = entries[e : e + 1, :] * page_len
        high = low + jnp.clip(lengths - e * page_len, 0, page_len)
        seen = seen + jnp.where((token >= low) & (token < high), 1.0, 0.0)
    return jnp.where(seen > 0.0, jnp.log2(jnp.maximum(seen, 1.0)), HIDDEN)


def identity(rows, on, off):
    across = lax.broadcasted_iota(jnp.int32, (rows, rows), 1)
    down = lax.broadcasted_iota(jnp.int32, (rows, rows), 0)
    return jnp.where(across == down, on, off)


def fill_queries(wide_query_ref, rows):
    ones = identity(rows, BIAS_UNIT, 0.0).astype(jnp.bfloat16)
    for h in range(wide_query_ref.shape[0] // rows):
        wide_query_ref[h * rows : (h + 1) * rows, HEAD_SIZE:] = ones


def fill_keys(wide_key_ref, entries_ref, length_ref, first_token, tokens, page_len):
    for start in range(0, tokens, TOKEN_STEP):
        size = min(TOKEN_STEP, tokens - start)
        bias = token_bias(entries_ref[...], length_ref[...], first_token + start, size, page_len)
        wide_key_ref[start : start + size, HEAD_SIZE:] = bias.astype(jnp.bfloat16)


def score_block(block, wide_query_ref, wide_key_ref, score_ref):
    tokens = score_ref.shape[1]
    top = None
    for start in range(0, tokens, TOKEN_STEP):
        size = min(TOKEN_STEP, tokens - start)
        part = lax.dot_general(
            wide_query_ref[block, :],
            wide_key_ref[start : start + size, :],
            (((1,), (1,)), ((), ())),
            preferred_element_type=jnp.float32,
        )
        score_ref[block, start : start + size] = part
        for lane in range(0, size, LANES):
            piece = part[:, lane : lane + LANES]
            top = piece if top is None else jnp.maximum(top, piece)
    return jnp.max(top, axis=1, keepdims=True)


def weigh_block(block, top, score_ref, weight_ref, wide_value_ref):
    tokens = score_ref.shape[1]
    for start in range(0, tokens, TOKEN_STEP):
        size = min(TOKEN_STEP, tokens - start)
        weights = jnp.exp2((score_ref[block, start : start + size] - top) * SCORE_SCALE)
        weight_ref[block, start : start + size] = weights.astype(jnp.bfloat16)
    return jnp.dot(weight_ref[block, :], wide_value_ref[...], preferred_element_type=jnp.float32)


def load_heads(wide_query_ref, query_ref):
    rows = query_ref.shape[0]
    for h in range(QUERY_GROUP):
        wide_query_ref[h * rows : (h + 1) * rows, :HEAD_SIZE] = query_ref[
            :, h * HEAD_SIZE : (h + 1) * HEAD_SIZE
        ]


def pool_kernel(page_len, query_ref, pool_ref, entries_ref, length_ref, part_ref, stat_ref, *refs):
    wide_query_ref, wide_key_ref, wide_value_ref, score_ref, weight_ref = refs
    rows = query_ref.shape[0]
    tokens = pool_ref.shape[0]

    @pl.when(pl.program_id(0) == 0)
    def _():
        fill_queries(wide_query_ref, rows)
        fill_keys(wide_key_ref, entries_ref, length_ref, 0, tokens, page_len)
        wide_value_ref[:, HEAD_SIZE:] = jnp.ones((tokens, HEAD_SIZE), jnp.bfloat16)

    wide_key_ref[:, :HEAD_SIZE] = pool_ref[:, :HEAD_SIZE]
    wide_value_ref[:, :HEAD_SIZE] = pool_ref[:, HEAD_SIZE:]
    load_heads(wide_query_ref, query_ref)
    lane = lax.broadcasted_iota(jnp.int32, (rows, LANES), 1)
    stats = jnp.zeros((rows, LANES), jnp.float32)
    for h in range(0, QUERY_GROUP, HEADS_STEP):
        block = slice(h * rows, (h + HEADS_STEP) * rows)
        top = score_block(block, wide_query_ref, wide_key_ref, score_ref)
        parts = weigh_block(block, top, score_ref, weight_ref, wide_value_ref)
        total = parts[:, HEAD_SIZE:]
        part_ref[block, :] = (parts[:, :HEAD_SIZE] / total).astype(jnp.bfloat16)
        level = top + jnp.log2(total) * (1.0 / SCORE_SCALE)
        for step in range(HEADS_STEP):
            own = slice(step * rows, (step + 1) * rows)
            stats = jnp.where(lane == h + step, level[own], stats)
    stat_ref[...] = stats


def attend_pool(queries, pool, entries, lengths, page_len):
    rows, width = queries.shape
    tokens = pool.shape[0]
    kv_local = pool.shape[1] // (2 * HEAD_SIZE)
    stacked = QUERY_GROUP * rows
    return pl.pallas_call(
        functools.partial(pool_kernel, page_len),
        grid=(kv_local,),
        out_shape=[
            jax.ShapeDtypeStruct((kv_local * stacked, LANES), jnp.bfloat16),
            jax.ShapeDtypeStruct((rows, kv_local * LANES), jnp.float32),
        ],
        in_specs=[
            pl.BlockSpec((rows, width // kv_local), lambda g: (0, g)),
            pl.BlockSpec((tokens, 2 * HEAD_SIZE), lambda g: (0, g)),
            whole(entries),
            whole(lengths),
        ],
        out_specs=[
            pl.BlockSpec((stacked, LANES), lambda g: (g, 0)),
            pl.BlockSpec((rows, LANES), lambda g: (0, g)),
        ],
        scratch_shapes=[
            pltpu.VMEM((stacked, 2 * HEAD_SIZE), jnp.bfloat16),
            pltpu.VMEM((tokens, 2 * HEAD_SIZE), jnp.bfloat16),
            pltpu.VMEM((tokens, 2 * HEAD_SIZE), jnp.bfloat16),
            pltpu.VMEM((stacked, tokens), jnp.float32),
            pltpu.VMEM((stacked, tokens), jnp.bfloat16),
        ],
        compiler_params=params(),
        cost_estimate=pl.CostEstimate(10**9, 10**7, 10**6),
        name="attend_pool",
    )(queries, pool, entries, lengths)


def finish_kernel(
    page_len,
    first_token,
    place,
    where_ref,
    query_ref,
    part_ref,
    stat_ref,
    arrived_ref,
    fresh_ref,
    entries_ref,
    length_ref,
    target_ref,
    position_ref,
    slot_ref,
    *refs,
):
    out_refs, refs = refs[:-6], refs[-6:]
    wide_query_ref, wide_key_ref, wide_value_ref, score_ref, weight_ref, heads_ref = refs
    rows = query_ref.shape[0]
    g = pl.program_id(0)
    tokens = arrived_ref.shape[0]

    @pl.when(g == 0)
    def _():
        fill_queries(wide_query_ref, rows)
        fill_keys(wide_key_ref, entries_ref, length_ref, first_token, tokens, page_len)
        wide_key_ref[tokens:, HEAD_SIZE:] = identity(rows, 0.0, HIDDEN).astype(jnp.bfloat16)
        wide_value_ref[:, HEAD_SIZE:] = jnp.ones((tokens + rows, HEAD_SIZE), jnp.bfloat16)

    for shelf, first in ((arrived_ref, 0), (fresh_ref, tokens)):
        own = slice(first, first + shelf.shape[0])
        wide_key_ref[own, :HEAD_SIZE] = shelf[:, :HEAD_SIZE]
        wide_value_ref[own, :HEAD_SIZE] = shelf[:, HEAD_SIZE:]
    load_heads(wide_query_ref, query_ref)
    for h in range(0, QUERY_GROUP, HEADS_STEP):
        block = slice(h * rows, (h + HEADS_STEP) * rows)
        level = jnp.concatenate(
            [stat_ref[:, h + step : h + step + 1] for step in range(HEADS_STEP)], axis=0
        )
        top = jnp.maximum(score_block(block, wide_query_ref, wide_key_ref, score_ref), level)
        parts = weigh_block(block, top, score_ref, weight_ref, wide_value_ref)
        pool_weight = jnp.exp2((level - top) * SCORE_SCALE)
        heads = parts[:, :HEAD_SIZE] + pool_weight * part_ref[block, :].astype(jnp.float32)
        heads = (heads / (parts[:, HEAD_SIZE:] + pool_weight)).astype(jnp.bfloat16)
        for step in range(HEADS_STEP):
            heads_ref[g, :, (h + step) * HEAD_SIZE : (h + step + 1) * HEAD_SIZE] = heads[
                step * rows : (step + 1) * rows
            ]

    @pl.when(g == pl.num_programs(0) - 1)
    def _():
        targets = target_ref[...]
        across = lax.broadcasted_iota(jnp.int32, (rows, rows), 1)
        down = lax.broadcasted_iota(jnp.int32, (rows, rows), 0)
        earlier = (row_to_column(targets) == targets) & (down < across)
        rank = jnp.sum(earlier.astype(jnp.int32), axis=0, keepdims=True)
        slots_of = place(targets, where_ref[0]) + rank
        slot_ref[...] = slots_of
        wide = heads_ref.shape[2]
        first = 0
        for out_ref in out_refs:
            slots = out_ref.shape[0]
            slot = first + lax.broadcasted_iota(jnp.int32, (slots, rows), 0)
            pick = slot == slots_of
            label = jnp.sum(jnp.where(pick, position_ref[...], 0), axis=1, keepdims=True)
            pick = pick.astype(jnp.float32).astype(jnp.bfloat16)
            for kv in range(heads_ref.shape[0]):
                out_ref[:, kv * wide : (kv + 1) * wide] = jnp.dot(
                    pick, heads_ref[kv], preferred_element_type=jnp.float32
                ).astype(jnp.bfloat16)
            out_ref[:, heads_ref.shape[0] * wide :] = jnp.broadcast_to(
                label.astype(jnp.float32).astype(jnp.bfloat16), (slots, LANES)
            )
            first += slots


def finish(
    where, queries, found, arrived, fresh, entries, lengths, targets, positions, page_len, first_token, blocks, place
):
    rows, width = queries.shape
    kv_local = arrived.shape[1] // (2 * HEAD_SIZE)
    tokens = arrived.shape[0] + rows
    stacked = QUERY_GROUP * rows
    shelf = lambda array: pl.BlockSpec((array.shape[0], 2 * HEAD_SIZE), lambda g: (0, g))
    small = (entries, lengths, targets, positions)
    out_shape = [jax.ShapeDtypeStruct((1, rows), jnp.int32)]
    out_shape += [jax.ShapeDtypeStruct((block, width + LANES), jnp.bfloat16) for block in blocks]
    return pl.pallas_call(
        functools.partial(finish_kernel, page_len, first_token, place),
        grid=(kv_local,),
        out_shape=out_shape,
        in_specs=[
            smem_spec(),
            pl.BlockSpec((rows, width // kv_local), lambda g: (0, g)),
            pl.BlockSpec((stacked, LANES), lambda g: (g, 0)),
            pl.BlockSpec((rows, LANES), lambda g: (0, g)),
        ]
        + [shelf(array) for array in (arrived, fresh)]
        + [whole(array) for array in small],
        out_specs=[whole(block) for block in out_shape],
        scratch_shapes=[
            pltpu.VMEM((stacked, 2 * HEAD_SIZE), jnp.bfloat16),
            pltpu.VMEM((tokens, 2 * HEAD_SIZE), jnp.bfloat16),
            pltpu.VMEM((tokens, 2 * HEAD_SIZE), jnp.bfloat16),
            pltpu.VMEM((stacked, tokens), jnp.float32),
            pltpu.VMEM((stacked, tokens), jnp.bfloat16),
            pltpu.VMEM((kv_local, rows, width // kv_local), jnp.bfloat16),
        ],
        compiler_params=params(12 + tokens * stacked * 7 // MIB),
        cost_estimate=cost(),
        name="finish",
    )(where, queries, *found, arrived, fresh, *small)


def after_kernel(*refs):
    pass


def after(arrays, *others):
    hbm = pl.BlockSpec(memory_space=pl.ANY)
    return pl.pallas_call(
        after_kernel,
        out_shape=[jax.ShapeDtypeStruct(array.shape, array.dtype) for array in arrays],
        in_specs=[hbm] * (len(arrays) + len(others)),
        out_specs=[hbm] * len(arrays),
        input_output_aliases={i: i for i in range(len(arrays))},
        compiler_params=params(1),
        cost_estimate=cost(),
        name="after",
    )(*arrays, *others)


def down_kernel(half_ref, *refs):
    block_refs, (own_ref, first_ref, second_ref, out_ref, rows_ref) = refs[:-5], refs[-5:]
    cap = out_ref.shape[0] // 8
    width = own_ref.shape[1]
    for b, block in enumerate(block_refs):
        rows_ref[b * cap : (b + 1) * cap, :] = block[:cap, :]
        rows_ref[(b + 4) * cap : (b + 5) * cap, :] = block[cap:, :]
    swapped = half_ref[0] == 1
    zero = jnp.where(swapped, second_ref[...], first_ref[...])
    one = jnp.where(swapped, first_ref[...], second_ref[...])
    lane = lax.broadcasted_iota(jnp.int32, (1, out_ref.shape[1]), 1)
    adapter = jnp.where(lane < out_ref.shape[1] // 2, 0.0, 1.0)
    for start, weights in ((0, own_ref[...]), (4 * cap, jnp.concatenate([zero, one], axis=0))):
        part = slice(start, start + 4 * cap)
        product = lax.dot_general(
            rows_ref[part, :width],
            weights,
            (((1,), (1,)), ((), ())),
            preferred_element_type=jnp.float32,
        )
        label = rows_ref[part, width:].astype(jnp.float32)
        out_ref[part, :] = jnp.where(label == adapter, product, 0.0)


def low_products(half, blocks, own, first, second):
    rows = sum(block.shape[0] for block in blocks)
    inputs = (*blocks, own, first, second)
    out_shape = jax.ShapeDtypeStruct((rows, own.shape[0]), jnp.float32)
    return pl.pallas_call(
        down_kernel,
        grid=(1,),
        out_shape=out_shape,
        in_specs=[smem_spec()]
        + [whole(array) for array in (*blocks, own)]
        + [pl.BlockSpec((first.shape[0], own.shape[1]), lambda *step: (0, 0))] * 2,
        out_specs=whole(out_shape),
        scratch_shapes=[pltpu.VMEM((rows, blocks[0].shape[1]), jnp.bfloat16)],
        compiler_params=params(),
        cost_estimate=cost(),
        name="low_products",
    )(half, *inputs)


def lift(low_refs, weights, out_refs):
    low = (low_refs[0][...] + low_refs[1][...]).astype(jnp.bfloat16)
    lifted = jnp.dot(low, weights, preferred_element_type=jnp.float32).astype(jnp.bfloat16)
    cap = out_refs[0].shape[0]
    for b, out_ref in enumerate(out_refs):
        out_ref[...] = lifted[b * cap : (b + 1) * cap]


def lift_own_kernel(mine_ref, other_ref, own_ref, *out_refs):
    lift((mine_ref, other_ref), own_ref[...], out_refs)


def lift_own(mine, other, weights):
    rows, rank = mine.shape
    width = weights.shape[1]
    step = 1024
    low = pl.BlockSpec((rows // 2, rank), lambda j: (0, 0))
    out = jax.ShapeDtypeStruct((rows // 8, width), jnp.bfloat16)
    return pl.pallas_call(
        lift_own_kernel,
        grid=(width // step,),
        out_shape=(out,) * 4,
        in_specs=[low, low, pl.BlockSpec((rank, step), lambda j: (0, j))],
        out_specs=[pl.BlockSpec((rows // 8, step), lambda j: (0, j))] * 4,
        compiler_params=params(),
        cost_estimate=cost(),
        name="lift_own",
    )(mine, other, weights)


def lift_far_kernel(half_ref, mine_ref, other_ref, first_ref, second_ref, *out_refs):
    low = (mine_ref[...] + other_ref[...]).astype(jnp.bfloat16)
    swapped = half_ref[0] == 1
    cap = out_refs[0].shape[0]
    zero = jnp.where(swapped, second_ref[...], first_ref[...])
    one = jnp.where(swapped, first_ref[...], second_ref[...])
    lifted = jnp.dot(
        low, jnp.concatenate([zero, one], axis=0), preferred_element_type=jnp.float32
    ).astype(jnp.bfloat16)
    for b, out_ref in enumerate(out_refs):
        out_ref[...] = lifted[b * cap : (b + 1) * cap]


def lift_far(half, mine, other, first, second):
    rows, rank = mine.shape
    width = first.shape[1]
    step = 1024
    low = pl.BlockSpec((rows // 2, rank), lambda j: (1, 0))
    out = jax.ShapeDtypeStruct((rows // 8, width), jnp.bfloat16)
    return pl.pallas_call(
        lift_far_kernel,
        grid=(width // step,),
        out_shape=(out,) * 4,
        in_specs=[smem_spec(), low, low] + [pl.BlockSpec((rank // 2, step), lambda j: (0, j))] * 2,
        out_specs=[pl.BlockSpec((rows // 8, step), lambda j: (0, j))] * 4,
        compiler_params=params(),
        cost_estimate=cost(),
        name="lift_far",
    )(half, mine, other, first, second)


def gather_rows_kernel(slot_ref, *refs):
    out_ref = refs[-1]
    rows = out_ref.shape[0]
    stacked = jnp.concatenate([ref[...] for ref in refs[:-1]], axis=0)
    slot = lax.broadcasted_iota(jnp.int32, (rows, stacked.shape[0]), 1)
    pick = (slot == row_to_column(slot_ref[...])).astype(jnp.float32).astype(jnp.bfloat16)
    out_ref[...] = jnp.dot(pick, stacked, preferred_element_type=jnp.float32).astype(jnp.bfloat16)


def gather_rows(slots, blocks):
    rows = slots.shape[1]
    width = blocks[0].shape[1]
    step = 1024
    return pl.pallas_call(
        gather_rows_kernel,
        grid=(width // step,),
        out_shape=jax.ShapeDtypeStruct((rows, width), jnp.bfloat16),
        in_specs=[pl.BlockSpec(slots.shape, lambda j: (0, 0))]
        + [pl.BlockSpec((block.shape[0], step), lambda j: (0, j)) for block in blocks],
        out_specs=pl.BlockSpec((rows, step), lambda j: (0, j)),
        compiler_params=params(),
        cost_estimate=cost(),
        name="gather_rows",
    )(slots, *blocks)


def along(array, group_bit, replica_bits):
    groups, replicas = lax.axis_size("group"), lax.axis_size("rep")
    pairs = [
        (g * replicas + r, (g ^ group_bit) * replicas + (r ^ replica_bits))
        for g in range(groups)
        for r in range(replicas)
    ]
    return lax.ppermute(array, ("group", "rep"), pairs)


def shared_local(
    queries,
    current_key_value,
    key_value_pool,
    request_page_entries,
    context_length,
    migration_page,
    migration_target,
    adapter_replica,
    adapter_position,
    adapter_down_weight,
    adapter_up_weight,
):
    rows, width = queries.shape
    replicas = lax.axis_size("rep")
    cap = 2 * rows // replicas
    group = lax.axis_index("group")
    half = group.reshape(1).astype(jnp.int32)
    where = jnp.stack([lax.axis_index("rep"), group]).astype(jnp.int32)
    targets = adapter_replica.reshape(1, -1)
    down_rows = jnp.swapaxes(adapter_down_weight, 1, 2)
    down = down_rows.reshape(-1, width)
    up = adapter_up_weight.reshape(-1, adapter_up_weight.shape[2])
    entries = request_page_entries.T
    lengths = context_length.reshape(1, -1)
    positions = adapter_position.reshape(1, -1)
    pages, page_len, features = key_value_pool.shape
    pool = key_value_pool.reshape(pages * page_len, features)

    columns = up.shape[1]
    rank = up.shape[0] // 2
    outgoing, *packs = outgoing_pages(
        half,
        migration_page,
        migration_target,
        key_value_pool,
        replicas,
        (down_rows, adapter_up_weight),
        (((0, width, 0, 0),), ((0, columns, 1, 0),)),
        ((rank, width), (rank, columns)),
    )
    arrived = lax.all_to_all(outgoing, "rep", split_axis=0, concat_axis=0, tiled=True)
    found = attend_pool(queries, pool, entries, lengths, page_len)
    first = [along(pack, 0, 4) for pack in after(packs, arrived, found[1])]

    def place(targets, replica):
        apart = jnp.bitwise_xor(targets, replica)
        return (2 * jnp.bitwise_and(apart, 3) + jnp.right_shift(apart, 2)) * cap

    slots, here, *outbound = finish(
        where,
        queries,
        found,
        arrived.reshape(-1, features),
        current_key_value,
        entries,
        lengths,
        targets,
        positions,
        page_len,
        pages * page_len,
        (2 * cap,) * 4,
        place,
    )
    blocks = [here] + [along(block, 0, b + 1) for b, block in enumerate(outbound)]
    second = [along(*after([first[0]], slots), 1, 0)]
    mine = low_products(half, blocks, down, first[0], second[0])
    second.append(along(*after([first[1]], mine), 1, 0))
    other = lax.ppermute(mine, "tp", [(0, 1), (1, 0)])
    own = lift_own(mine, other, up)
    own = [block if b == 0 else along(block, 0, b) for b, block in enumerate(own)]
    far = lift_far(half, mine, other, first[1], second[1])
    far = [block if b == 0 else along(block, 0, b) for b, block in enumerate(far)]
    return gather_rows(slots, [block for pair in zip(own, far) for block in pair])


def local(
    queries,
    current_key_value,
    key_value_pool,
    request_page_entries,
    context_length,
    migration_page,
    migration_target,
    adapter_replica,
    adapter_position,
    adapter_down_weight,
    adapter_up_weight,
):
    replicas = lax.axis_size("rep")
    if replicas == 8 and lax.axis_size("group") == 2 and adapter_down_weight.shape[0] == 2:
        return shared_local(
            queries,
            current_key_value,
            key_value_pool,
            request_page_entries,
            context_length,
            migration_page,
            migration_target,
            adapter_replica,
            adapter_position,
            adapter_down_weight,
            adapter_up_weight,
        )
    rows, width = queries.shape
    adapter_number = adapter_down_weight.shape[0]
    slot_cap = max(2, (2 * rows + replicas - 1) // replicas)
    entries = request_page_entries.T
    lengths = context_length.reshape(1, -1)
    pages, page_len, features = key_value_pool.shape
    pool = key_value_pool.reshape(pages * page_len, features)
    where = jnp.stack([lax.axis_index("rep"), lax.axis_index("group")]).astype(jnp.int32)
    (outgoing,) = outgoing_pages(where, migration_page, migration_target, key_value_pool, replicas)
    arrived = lax.all_to_all(outgoing, "rep", split_axis=0, concat_axis=0, tiled=True)
    found = attend_pool(queries, pool, entries, lengths, page_len)
    slots, outbound = finish(
        where,
        queries,
        found,
        arrived.reshape(-1, features),
        current_key_value,
        entries,
        lengths,
        adapter_replica.reshape(1, -1),
        adapter_position.reshape(1, -1),
        page_len,
        pages * page_len,
        (replicas * slot_cap,),
        lambda targets, replica: targets * slot_cap,
    )
    outbound = outbound.reshape(replicas, slot_cap, -1)
    activations = lax.all_to_all(outbound, "rep", split_axis=0, concat_axis=0, tiled=True)
    shape_in = activations.shape
    flat_output = activations.reshape(-1, shape_in[2])
    selector = (
        flat_output[:, width : width + 1].astype(jnp.int32)
        == jnp.arange(adapter_number, dtype=jnp.int32)[None, :]
    )
    reduced_rank_total = jnp.einsum(
        "oh,pht->opt", flat_output[:, :width], adapter_down_weight, preferred_element_type=jnp.float32
    )
    partial_low = jnp.sum(jnp.where(selector[:, :, None], reduced_rank_total, 0.0), axis=1)
    low_rank = lax.psum(partial_low, "tp").astype(jnp.bfloat16)
    broadcast_result = jnp.where(
        selector[:, :, None], low_rank[:, None, :], jnp.zeros((), jnp.bfloat16)
    )
    broadcast_result = broadcast_result.reshape(flat_output.shape[0], -1)
    lifted = jnp.dot(
        broadcast_result,
        adapter_up_weight.reshape(-1, adapter_up_weight.shape[2]),
        preferred_element_type=jnp.float32,
    )
    lifted = lifted.astype(jnp.bfloat16).reshape(shape_in[0], shape_in[1], -1)
    returned = lax.all_to_all(lifted, "rep", split_axis=0, concat_axis=0, tiled=True)
    route_mask = (
        jnp.arange(replicas * slot_cap, dtype=jnp.int32)[:, None] == slots
    ).astype(jnp.bfloat16)
    delta = jnp.einsum(
        "sr,sd->rd",
        route_mask,
        returned.reshape(replicas * slot_cap, -1),
        preferred_element_type=jnp.float32,
    )
    return delta.astype(jnp.bfloat16)


def solution(mesh):
    return jax.shard_map(
        local,
        mesh=mesh,
        in_specs=(
            P(("group", "rep"), "tp"),
            P(("group", "rep"), "tp"),
            P(("group", "rep"), None, "tp"),
            P(("group", "rep"), None),
            P(("group", "rep")),
            P(("group", "rep")),
            P(("group", "rep")),
            P(("group", "rep"), None),
            P(("group", "rep")),
            P("rep", "tp", None),
            P("rep", None, "tp"),
        ),
        out_specs=P(("group", "rep"), "tp"),
        check_vma=False,
    )
```

```python
import functools
import math

import jax
import jax.numpy as jnp
from jax import lax
from jax.experimental import pallas as pl
from jax.experimental.pallas import tpu as pltpu
from jax.sharding import PartitionSpec as P

HEAD_SIZE = 128
QUERY_GROUP = 8
MCAP = 2
LANES = 128
TOKEN_STEP = 256
HIDDEN = -1e30
SCORE_SCALE = math.log2(math.e) / math.sqrt(HEAD_SIZE)
BIAS_UNIT = float(jnp.bfloat16(1.0 / SCORE_SCALE))
HEADS_STEP = 2
MIB = 1024 * 1024


def whole(array):
    shape = array.shape
    return pl.BlockSpec(shape, lambda *step: (0,) * len(shape))


def smem_spec():
    return pl.BlockSpec(memory_space=pltpu.SMEM)


def params(mebibytes=24):
    return pltpu.CompilerParams(vmem_limit_bytes=mebibytes * MIB)


def cost():
    return pl.CostEstimate(flops=1024, bytes_accessed=1024, transcendentals=0)


def row_to_column(row):
    count = row.shape[1]
    across = lax.broadcasted_iota(jnp.int32, (count, count), 1)
    down = lax.broadcasted_iota(jnp.int32, (count, count), 0)
    return jnp.sum(jnp.where(across == down, row, 0), axis=1, keepdims=True)


def outgoing_kernel(pieces, half_ref, page_ref, target_ref, pool_ref, *refs):
    count_ref, chosen_ref, page_sem, share_sem = refs[-4:]
    out_ref, share_refs, mine_refs = refs[len(pieces)], refs[: len(pieces)], refs[len(pieces) + 1 : -4]
    entry_number = page_ref.shape[0]
    slot_number = out_ref.shape[0]

    def clear(slot, carry):
        chosen_ref[slot] = 0
        count_ref[slot // MCAP] = 0
        return carry

    def place(entry, carry):
        target = target_ref[entry]
        rank = count_ref[target]
        chosen_ref[target * MCAP + rank] = page_ref[entry]
        count_ref[target] = rank + 1
        return carry

    def page_copy(slot):
        return pltpu.make_async_copy(
            pool_ref.at[chosen_ref[slot]], out_ref.at[slot], page_sem.at[slot]
        )

    def send(slot, carry):
        page_copy(slot).start()
        return carry

    def finish(slot, carry):
        page_copy(slot).wait()
        return carry

    shares = []
    for share, cuts in zip(share_refs, pieces):
        for first, last, pack, start in cuts:
            shares.append(
                pltpu.make_async_copy(
                    share.at[half_ref[0], :, pl.ds(first, last - first)],
                    mine_refs[pack].at[:, pl.ds(start, last - first)],
                    share_sem.at[len(shares)],
                )
            )
    lax.fori_loop(0, slot_number, clear, 0)
    lax.fori_loop(0, entry_number, place, 0)
    lax.fori_loop(0, slot_number, send, 0)
    for share in shares:
        share.start()
    lax.fori_loop(0, slot_number, finish, 0)
    for share in shares:
        share.wait()


def outgoing_pages(half, migration_page, migration_target, pool, replicas, shares=(), pieces=(), packs=()):
    slots = replicas * MCAP
    hbm = pl.BlockSpec(memory_space=pltpu.HBM)
    out_shape = [jax.ShapeDtypeStruct((slots,) + pool.shape[1:], pool.dtype)]
    out_shape += [jax.ShapeDtypeStruct(pack, pool.dtype) for pack in packs]
    return pl.pallas_call(
        functools.partial(outgoing_kernel, pieces),
        out_shape=out_shape,
        in_specs=[smem_spec()] * 3 + [hbm] * (1 + len(shares)),
        out_specs=[whole(out) for out in out_shape],
        scratch_shapes=[
            pltpu.SMEM((replicas,), jnp.int32),
            pltpu.SMEM((slots,), jnp.int32),
            pltpu.SemaphoreType.DMA((slots,)),
            pltpu.SemaphoreType.DMA((max(1, sum(len(cuts) for cuts in pieces)),)),
        ],
        compiler_params=params(60),
        cost_estimate=cost(),
        name="outgoing_pages",
    )(half, migration_page, migration_target, pool, *shares)


def token_bias(entries, lengths, first_token, tokens, page_len):
    shape = (tokens, entries.shape[1])
    token = first_token + lax.broadcasted_iota(jnp.int32, shape, 0)
    seen = jnp.zeros(shape, jnp.float32)
    for e in range(entries.shape[0]):
        low = entries[e : e + 1, :] * page_len
        high = low + jnp.clip(lengths - e * page_len, 0, page_len)
        seen = seen + jnp.where((token >= low) & (token < high), 1.0, 0.0)
    return jnp.where(seen > 0.0, jnp.log2(jnp.maximum(seen, 1.0)), HIDDEN)


def identity(rows, on, off):
    across = lax.broadcasted_iota(jnp.int32, (rows, rows), 1)
    down = lax.broadcasted_iota(jnp.int32, (rows, rows), 0)
    return jnp.where(across == down, on, off)


def fill_queries(wide_query_ref, rows):
    ones = identity(rows, BIAS_UNIT, 0.0).astype(jnp.bfloat16)
    for h in range(wide_query_ref.shape[0] // rows):
        wide_query_ref[h * rows : (h + 1) * rows, HEAD_SIZE:] = ones


def fill_keys(wide_key_ref, entries_ref, length_ref, first_token, tokens, page_len):
    for start in range(0, tokens, TOKEN_STEP):
        size = min(TOKEN_STEP, tokens - start)
        bias = token_bias(entries_ref[...], length_ref[...], first_token + start, size, page_len)
        wide_key_ref[start : start + size, HEAD_SIZE:] = bias.astype(jnp.bfloat16)


def score_block(block, wide_query_ref, wide_key_ref, score_ref):
    tokens = score_ref.shape[1]
    top = None
    for start in range(0, tokens, TOKEN_STEP):
        size = min(TOKEN_STEP, tokens - start)
        part = lax.dot_general(
            wide_query_ref[block, :],
            wide_key_ref[start : start + size, :],
            (((1,), (1,)), ((), ())),
            preferred_element_type=jnp.float32,
        )
        score_ref[block, start : start + size] = part
        for lane in range(0, size, LANES):
            piece = part[:, lane : lane + LANES]
            top = piece if top is None else jnp.maximum(top, piece)
    return jnp.max(top, axis=1, keepdims=True)


def weigh_block(block, top, score_ref, weight_ref, wide_value_ref):
    tokens = score_ref.shape[1]
    for start in range(0, tokens, TOKEN_STEP):
        size = min(TOKEN_STEP, tokens - start)
        weights = jnp.exp2((score_ref[block, start : start + size] - top) * SCORE_SCALE)
        weight_ref[block, start : start + size] = weights.astype(jnp.bfloat16)
    return jnp.dot(weight_ref[block, :], wide_value_ref[...], preferred_element_type=jnp.float32)


def load_heads(wide_query_ref, query_ref):
    rows = query_ref.shape[0]
    for h in range(QUERY_GROUP):
        wide_query_ref[h * rows : (h + 1) * rows, :HEAD_SIZE] = query_ref[
            :, h * HEAD_SIZE : (h + 1) * HEAD_SIZE
        ]


def pool_kernel(page_len, query_ref, pool_ref, entries_ref, length_ref, part_ref, stat_ref, *refs):
    wide_query_ref, wide_key_ref, wide_value_ref, score_ref, weight_ref = refs
    rows = query_ref.shape[0]
    tokens = pool_ref.shape[0]

    @pl.when(pl.program_id(0) == 0)
    def _():
        fill_queries(wide_query_ref, rows)
        fill_keys(wide_key_ref, entries_ref, length_ref, 0, tokens, page_len)
        wide_value_ref[:, HEAD_SIZE:] = jnp.ones((tokens, HEAD_SIZE), jnp.bfloat16)

    wide_key_ref[:, :HEAD_SIZE] = pool_ref[:, :HEAD_SIZE]
    wide_value_ref[:, :HEAD_SIZE] = pool_ref[:, HEAD_SIZE:]
    load_heads(wide_query_ref, query_ref)
    lane = lax.broadcasted_iota(jnp.int32, (rows, LANES), 1)
    stats = jnp.zeros((rows, LANES), jnp.float32)
    for h in range(0, QUERY_GROUP, HEADS_STEP):
        block = slice(h * rows, (h + HEADS_STEP) * rows)
        top = score_block(block, wide_query_ref, wide_key_ref, score_ref)
        parts = weigh_block(block, top, score_ref, weight_ref, wide_value_ref)
        total = parts[:, HEAD_SIZE:]
        part_ref[block, :] = (parts[:, :HEAD_SIZE] / total).astype(jnp.bfloat16)
        level = top + jnp.log2(total) * (1.0 / SCORE_SCALE)
        for step in range(HEADS_STEP):
            own = slice(step * rows, (step + 1) * rows)
            stats = jnp.where(lane == h + step, level[own], stats)
    stat_ref[...] = stats


def attend_pool(queries, pool, entries, lengths, page_len):
    rows, width = queries.shape
    tokens = pool.shape[0]
    kv_local = pool.shape[1] // (2 * HEAD_SIZE)
    stacked = QUERY_GROUP * rows
    return pl.pallas_call(
        functools.partial(pool_kernel, page_len),
        grid=(kv_local,),
        out_shape=[
            jax.ShapeDtypeStruct((kv_local * stacked, LANES), jnp.bfloat16),
            jax.ShapeDtypeStruct((rows, kv_local * LANES), jnp.float32),
        ],
        in_specs=[
            pl.BlockSpec((rows, width // kv_local), lambda g: (0, g)),
            pl.BlockSpec((tokens, 2 * HEAD_SIZE), lambda g: (0, g)),
            whole(entries),
            whole(lengths),
        ],
        out_specs=[
            pl.BlockSpec((stacked, LANES), lambda g: (g, 0)),
            pl.BlockSpec((rows, LANES), lambda g: (0, g)),
        ],
        scratch_shapes=[
            pltpu.VMEM((stacked, 2 * HEAD_SIZE), jnp.bfloat16),
            pltpu.VMEM((tokens, 2 * HEAD_SIZE), jnp.bfloat16),
            pltpu.VMEM((tokens, 2 * HEAD_SIZE), jnp.bfloat16),
            pltpu.VMEM((stacked, tokens), jnp.float32),
            pltpu.VMEM((stacked, tokens), jnp.bfloat16),
        ],
        compiler_params=params(),
        cost_estimate=pl.CostEstimate(10**9, 10**7, 10**6),
        name="attend_pool",
    )(queries, pool, entries, lengths)


def finish_kernel(
    page_len,
    first_token,
    place,
    where_ref,
    query_ref,
    part_ref,
    stat_ref,
    arrived_ref,
    fresh_ref,
    entries_ref,
    length_ref,
    target_ref,
    position_ref,
    slot_ref,
    *refs,
):
    out_refs, refs = refs[:-6], refs[-6:]
    wide_query_ref, wide_key_ref, wide_value_ref, score_ref, weight_ref, heads_ref = refs
    rows = query_ref.shape[0]
    g = pl.program_id(0)
    tokens = arrived_ref.shape[0]

    @pl.when(g == 0)
    def _():
        fill_queries(wide_query_ref, rows)
        fill_keys(wide_key_ref, entries_ref, length_ref, first_token, tokens, page_len)
        wide_key_ref[tokens:, HEAD_SIZE:] = identity(rows, 0.0, HIDDEN).astype(jnp.bfloat16)
        wide_value_ref[:, HEAD_SIZE:] = jnp.ones((tokens + rows, HEAD_SIZE), jnp.bfloat16)

    for shelf, first in ((arrived_ref, 0), (fresh_ref, tokens)):
        own = slice(first, first + shelf.shape[0])
        wide_key_ref[own, :HEAD_SIZE] = shelf[:, :HEAD_SIZE]
        wide_value_ref[own, :HEAD_SIZE] = shelf[:, HEAD_SIZE:]
    load_heads(wide_query_ref, query_ref)
    for h in range(0, QUERY_GROUP, HEADS_STEP):
        block = slice(h * rows, (h + HEADS_STEP) * rows)
        level = jnp.concatenate(
            [stat_ref[:, h + step : h + step + 1] for step in range(HEADS_STEP)], axis=0
        )
        top = jnp.maximum(score_block(block, wide_query_ref, wide_key_ref, score_ref), level)
        parts = weigh_block(block, top, score_ref, weight_ref, wide_value_ref)
        pool_weight = jnp.exp2((level - top) * SCORE_SCALE)
        heads = parts[:, :HEAD_SIZE] + pool_weight * part_ref[block, :].astype(jnp.float32)
        heads = (heads / (parts[:, HEAD_SIZE:] + pool_weight)).astype(jnp.bfloat16)
        for step in range(HEADS_STEP):
            heads_ref[g, :, (h + step) * HEAD_SIZE : (h + step + 1) * HEAD_SIZE] = heads[
                step * rows : (step + 1) * rows
            ]

    @pl.when(g == pl.num_programs(0) - 1)
    def _():
        targets = target_ref[...]
        across = lax.broadcasted_iota(jnp.int32, (rows, rows), 1)
        down = lax.broadcasted_iota(jnp.int32, (rows, rows), 0)
        earlier = (row_to_column(targets) == targets) & (down < across)
        rank = jnp.sum(earlier.astype(jnp.int32), axis=0, keepdims=True)
        slots_of = place(targets, where_ref[0]) + rank
        slot_ref[...] = slots_of
        wide = heads_ref.shape[2]
        first = 0
        for out_ref in out_refs:
            slots = out_ref.shape[0]
            slot = first + lax.broadcasted_iota(jnp.int32, (slots, rows), 0)
            pick = slot == slots_of
            label = jnp.sum(jnp.where(pick, position_ref[...], 0), axis=1, keepdims=True)
            pick = pick.astype(jnp.float32).astype(jnp.bfloat16)
            for kv in range(heads_ref.shape[0]):
                out_ref[:, kv * wide : (kv + 1) * wide] = jnp.dot(
                    pick, heads_ref[kv], preferred_element_type=jnp.float32
                ).astype(jnp.bfloat16)
            out_ref[:, heads_ref.shape[0] * wide :] = jnp.broadcast_to(
                label.astype(jnp.float32).astype(jnp.bfloat16), (slots, LANES)
            )
            first += slots


def finish(
    where, queries, found, arrived, fresh, entries, lengths, targets, positions, page_len, first_token, blocks, place
):
    rows, width = queries.shape
    kv_local = arrived.shape[1] // (2 * HEAD_SIZE)
    tokens = arrived.shape[0] + rows
    stacked = QUERY_GROUP * rows
    shelf = lambda array: pl.BlockSpec((array.shape[0], 2 * HEAD_SIZE), lambda g: (0, g))
    small = (entries, lengths, targets, positions)
    out_shape = [jax.ShapeDtypeStruct((1, rows), jnp.int32)]
    out_shape += [jax.ShapeDtypeStruct((block, width + LANES), jnp.bfloat16) for block in blocks]
    return pl.pallas_call(
        functools.partial(finish_kernel, page_len, first_token, place),
        grid=(kv_local,),
        out_shape=out_shape,
        in_specs=[
            smem_spec(),
            pl.BlockSpec((rows, width // kv_local), lambda g: (0, g)),
            pl.BlockSpec((stacked, LANES), lambda g: (g, 0)),
            pl.BlockSpec((rows, LANES), lambda g: (0, g)),
        ]
        + [shelf(array) for array in (arrived, fresh)]
        + [whole(array) for array in small],
        out_specs=[whole(block) for block in out_shape],
        scratch_shapes=[
            pltpu.VMEM((stacked, 2 * HEAD_SIZE), jnp.bfloat16),
            pltpu.VMEM((tokens, 2 * HEAD_SIZE), jnp.bfloat16),
            pltpu.VMEM((tokens, 2 * HEAD_SIZE), jnp.bfloat16),
            pltpu.VMEM((stacked, tokens), jnp.float32),
            pltpu.VMEM((stacked, tokens), jnp.bfloat16),
            pltpu.VMEM((kv_local, rows, width // kv_local), jnp.bfloat16),
        ],
        compiler_params=params(12 + tokens * stacked * 7 // MIB),
        cost_estimate=cost(),
        name="finish",
    )(where, queries, *found, arrived, fresh, *small)


def after_kernel(*refs):
    pass


def after(arrays, *others):
    hbm = pl.BlockSpec(memory_space=pl.ANY)
    return pl.pallas_call(
        after_kernel,
        out_shape=[jax.ShapeDtypeStruct(array.shape, array.dtype) for array in arrays],
        in_specs=[hbm] * (len(arrays) + len(others)),
        out_specs=[hbm] * len(arrays),
        input_output_aliases={i: i for i in range(len(arrays))},
        compiler_params=params(1),
        cost_estimate=cost(),
        name="after",
    )(*arrays, *others)


def down_kernel(half_ref, *refs):
    block_refs, (own_ref, first_ref, second_ref, out_ref, rows_ref) = refs[:-5], refs[-5:]
    cap = out_ref.shape[0] // 8
    width = own_ref.shape[1]
    for b, block in enumerate(block_refs):
        rows_ref[b * cap : (b + 1) * cap, :] = block[:cap, :]
        rows_ref[(b + 4) * cap : (b + 5) * cap, :] = block[cap:, :]
    swapped = half_ref[0] == 1
    zero = jnp.where(swapped, second_ref[...], first_ref[...])
    one = jnp.where(swapped, first_ref[...], second_ref[...])
    lane = lax.broadcasted_iota(jnp.int32, (1, out_ref.shape[1]), 1)
    adapter = jnp.where(lane < out_ref.shape[1] // 2, 0.0, 1.0)
    for start, weights in ((0, own_ref[...]), (4 * cap, jnp.concatenate([zero, one], axis=0))):
        part = slice(start, start + 4 * cap)
        product = lax.dot_general(
            rows_ref[part, :width],
            weights,
            (((1,), (1,)), ((), ())),
            preferred_element_type=jnp.float32,
        )
        label = rows_ref[part, width:].astype(jnp.float32)
        out_ref[part, :] = jnp.where(label == adapter, product, 0.0)


def low_products(half, blocks, own, first, second):
    rows = sum(block.shape[0] for block in blocks)
    inputs = (*blocks, own, first, second)
    out_shape = jax.ShapeDtypeStruct((rows, own.shape[0]), jnp.float32)
    return pl.pallas_call(
        down_kernel,
        grid=(1,),
        out_shape=out_shape,
        in_specs=[smem_spec()]
        + [whole(array) for array in (*blocks, own)]
        + [pl.BlockSpec((first.shape[0], own.shape[1]), lambda *step: (0, 0))] * 2,
        out_specs=whole(out_shape),
        scratch_shapes=[pltpu.VMEM((rows, blocks[0].shape[1]), jnp.bfloat16)],
        compiler_params=params(),
        cost_estimate=cost(),
        name="low_products",
    )(half, *inputs)


def lift(low_refs, weights, out_refs):
    low = (low_refs[0][...] + low_refs[1][...]).astype(jnp.bfloat16)
    lifted = jnp.dot(low, weights, preferred_element_type=jnp.float32).astype(jnp.bfloat16)
    cap = out_refs[0].shape[0]
    for b, out_ref in enumerate(out_refs):
        out_ref[...] = lifted[b * cap : (b + 1) * cap]


def lift_own_kernel(mine_ref, other_ref, own_ref, *out_refs):
    lift((mine_ref, other_ref), own_ref[...], out_refs)


def lift_own(mine, other, weights):
    rows, rank = mine.shape
    width = weights.shape[1]
    step = 1024
    low = pl.BlockSpec((rows // 2, rank), lambda j: (0, 0))
    out = jax.ShapeDtypeStruct((rows // 8, width), jnp.bfloat16)
    return pl.pallas_call(
        lift_own_kernel,
        grid=(width // step,),
        out_shape=(out,) * 4,
        in_specs=[low, low, pl.BlockSpec((rank, step), lambda j: (0, j))],
        out_specs=[pl.BlockSpec((rows // 8, step), lambda j: (0, j))] * 4,
        compiler_params=params(),
        cost_estimate=cost(),
        name="lift_own",
    )(mine, other, weights)


def lift_far_kernel(half_ref, mine_ref, other_ref, *refs):
    number = (len(refs) - 4) // 2
    first_refs, second_refs, out_refs = refs[:number], refs[number : 2 * number], refs[2 * number :]
    low = (mine_ref[...] + other_ref[...]).astype(jnp.bfloat16)
    swapped = half_ref[0] == 1
    cap = out_refs[0].shape[0]
    place = 0
    for first_ref, second_ref in zip(first_refs, second_refs):
        columns = slice(place, place + first_ref.shape[1])
        zero = jnp.where(swapped, second_ref[...], first_ref[...])
        one = jnp.where(swapped, first_ref[...], second_ref[...])
        lifted = jnp.dot(
            low, jnp.concatenate([zero, one], axis=0), preferred_element_type=jnp.float32
        ).astype(jnp.bfloat16)
        for b, out_ref in enumerate(out_refs):
            out_ref[:, columns] = lifted[b * cap : (b + 1) * cap]
        place = columns.stop


def lift_far(half, mine, other, first, second):
    rows, rank = mine.shape
    width = sum(piece.shape[1] for piece in first)
    low = pl.BlockSpec((rows // 2, rank), lambda j: (1, 0))
    out = jax.ShapeDtypeStruct((rows // 8, width), jnp.bfloat16)
    return pl.pallas_call(
        lift_far_kernel,
        grid=(1,),
        out_shape=(out,) * 4,
        in_specs=[smem_spec(), low, low] + [whole(piece) for piece in (*first, *second)],
        out_specs=[whole(out)] * 4,
        compiler_params=params(),
        cost_estimate=cost(),
        name="lift_far",
    )(half, mine, other, *first, *second)


def gather_rows_kernel(slot_ref, *refs):
    out_ref = refs[-1]
    rows = out_ref.shape[0]
    stacked = jnp.concatenate([ref[...] for ref in refs[:-1]], axis=0)
    slot = lax.broadcasted_iota(jnp.int32, (rows, stacked.shape[0]), 1)
    pick = (slot == row_to_column(slot_ref[...])).astype(jnp.float32).astype(jnp.bfloat16)
    out_ref[...] = jnp.dot(pick, stacked, preferred_element_type=jnp.float32).astype(jnp.bfloat16)


def gather_rows(slots, blocks):
    rows = slots.shape[1]
    width = blocks[0].shape[1]
    step = 2048
    return pl.pallas_call(
        gather_rows_kernel,
        grid=(width // step,),
        out_shape=jax.ShapeDtypeStruct((rows, width), jnp.bfloat16),
        in_specs=[pl.BlockSpec(slots.shape, lambda j: (0, 0))]
        + [pl.BlockSpec((block.shape[0], step), lambda j: (0, j)) for block in blocks],
        out_specs=pl.BlockSpec((rows, step), lambda j: (0, j)),
        compiler_params=params(),
        cost_estimate=cost(),
        name="gather_rows",
    )(slots, *blocks)


def along(array, group_bit, replica_bits):
    groups, replicas = lax.axis_size("group"), lax.axis_size("rep")
    pairs = [
        (g * replicas + r, (g ^ group_bit) * replicas + (r ^ replica_bits))
        for g in range(groups)
        for r in range(replicas)
    ]
    return lax.ppermute(array, ("group", "rep"), pairs)


def shared_local(
    queries,
    current_key_value,
    key_value_pool,
    request_page_entries,
    context_length,
    migration_page,
    migration_target,
    adapter_replica,
    adapter_position,
    adapter_down_weight,
    adapter_up_weight,
):
    rows, width = queries.shape
    replicas = lax.axis_size("rep")
    cap = 2 * rows // replicas
    group = lax.axis_index("group")
    half = group.reshape(1).astype(jnp.int32)
    where = jnp.stack([lax.axis_index("rep"), group]).astype(jnp.int32)
    targets = adapter_replica.reshape(1, -1)
    down_rows = jnp.swapaxes(adapter_down_weight, 1, 2)
    down = down_rows.reshape(-1, width)
    up = adapter_up_weight.reshape(-1, adapter_up_weight.shape[2])
    entries = request_page_entries.T
    lengths = context_length.reshape(1, -1)
    positions = adapter_position.reshape(1, -1)
    pages, page_len, features = key_value_pool.shape
    pool = key_value_pool.reshape(pages * page_len, features)

    columns = up.shape[1]
    early = columns // 8 * 4
    rank = up.shape[0] // 2
    outgoing, *packs = outgoing_pages(
        half,
        migration_page,
        migration_target,
        key_value_pool,
        replicas,
        (down_rows, adapter_up_weight),
        (((0, width, 0, 0),), ((0, early, 1, 0), (early, columns, 2, 0))),
        ((rank, width), (rank, early), (rank, columns - early)),
    )
    arrived = lax.all_to_all(outgoing, "rep", split_axis=0, concat_axis=0, tiled=True)
    found = attend_pool(queries, pool, entries, lengths, page_len)
    first = [along(pack, 0, 6) for pack in after(packs[:2], arrived, found[1])]

    def place(targets, replica):
        apart = jnp.bitwise_xor(targets, replica)
        far = jnp.right_shift(apart, 2)
        return (2 * jnp.bitwise_xor(jnp.bitwise_and(apart, 3), 2 * far) + far) * cap

    slots, here, *outbound = finish(
        where,
        queries,
        found,
        arrived.reshape(-1, features),
        current_key_value,
        entries,
        lengths,
        targets,
        positions,
        page_len,
        pages * page_len,
        (2 * cap,) * 4,
        place,
    )
    blocks = [along(block, 0, 3 - b) for b, block in enumerate(outbound[::-1])]
    blocks = [here] + blocks[::-1]
    first.append(along(*after([packs[2]], blocks[3]), 0, 6))
    second = [along(*after([first[0]], slots), 1, 0), along(*after([first[1]], blocks[1]), 1, 0)]
    mine = low_products(half, blocks, down, first[0], second[0])
    other = lax.ppermute(mine, "tp", [(0, 1), (1, 0)])
    second.append(along(*after([first[2]], other), 1, 0))
    own = lift_own(mine, other, up)
    own = [block if b == 0 else along(block, 0, b) for b, block in enumerate(own)]
    far = lift_far(half, mine, other, first[1:], second[1:])
    far = [block if b == 0 else along(block, 0, b) for b, block in enumerate(far)]
    return gather_rows(slots, [block for pair in zip(own, far) for block in pair])


def local(
    queries,
    current_key_value,
    key_value_pool,
    request_page_entries,
    context_length,
    migration_page,
    migration_target,
    adapter_replica,
    adapter_position,
    adapter_down_weight,
    adapter_up_weight,
):
    replicas = lax.axis_size("rep")
    if replicas == 8 and lax.axis_size("group") == 2 and adapter_down_weight.shape[0] == 2:
        return shared_local(
            queries,
            current_key_value,
            key_value_pool,
            request_page_entries,
            context_length,
            migration_page,
            migration_target,
            adapter_replica,
            adapter_position,
            adapter_down_weight,
            adapter_up_weight,
        )
    rows, width = queries.shape
    adapter_number = adapter_down_weight.shape[0]
    slot_cap = max(2, (2 * rows + replicas - 1) // replicas)
    entries = request_page_entries.T
    lengths = context_length.reshape(1, -1)
    pages, page_len, features = key_value_pool.shape
    pool = key_value_pool.reshape(pages * page_len, features)
    where = jnp.stack([lax.axis_index("rep"), lax.axis_index("group")]).astype(jnp.int32)
    (outgoing,) = outgoing_pages(where, migration_page, migration_target, key_value_pool, replicas)
    arrived = lax.all_to_all(outgoing, "rep", split_axis=0, concat_axis=0, tiled=True)
    found = attend_pool(queries, pool, entries, lengths, page_len)
    slots, outbound = finish(
        where,
        queries,
        found,
        arrived.reshape(-1, features),
        current_key_value,
        entries,
        lengths,
        adapter_replica.reshape(1, -1),
        adapter_position.reshape(1, -1),
        page_len,
        pages * page_len,
        (replicas * slot_cap,),
        lambda targets, replica: targets * slot_cap,
    )
    outbound = outbound.reshape(replicas, slot_cap, -1)
    activations = lax.all_to_all(outbound, "rep", split_axis=0, concat_axis=0, tiled=True)
    shape_in = activations.shape
    flat_output = activations.reshape(-1, shape_in[2])
    selector = (
        flat_output[:, width : width + 1].astype(jnp.int32)
        == jnp.arange(adapter_number, dtype=jnp.int32)[None, :]
    )
    reduced_rank_total = jnp.einsum(
        "oh,pht->opt", flat_output[:, :width], adapter_down_weight, preferred_element_type=jnp.float32
    )
    partial_low = jnp.sum(jnp.where(selector[:, :, None], reduced_rank_total, 0.0), axis=1)
    low_rank = lax.psum(partial_low, "tp").astype(jnp.bfloat16)
    broadcast_result = jnp.where(
        selector[:, :, None], low_rank[:, None, :], jnp.zeros((), jnp.bfloat16)
    )
    broadcast_result = broadcast_result.reshape(flat_output.shape[0], -1)
    lifted = jnp.dot(
        broadcast_result,
        adapter_up_weight.reshape(-1, adapter_up_weight.shape[2]),
        preferred_element_type=jnp.float32,
    )
    lifted = lifted.astype(jnp.bfloat16).reshape(shape_in[0], shape_in[1], -1)
    returned = lax.all_to_all(lifted, "rep", split_axis=0, concat_axis=0, tiled=True)
    route_mask = (
        jnp.arange(replicas * slot_cap, dtype=jnp.int32)[:, None] == slots
    ).astype(jnp.bfloat16)
    delta = jnp.einsum(
        "sr,sd->rd",
        route_mask,
        returned.reshape(replicas * slot_cap, -1),
        preferred_element_type=jnp.float32,
    )
    return delta.astype(jnp.bfloat16)


def solution(mesh):
    return jax.shard_map(
        local,
        mesh=mesh,
        in_specs=(
            P(("group", "rep"), "tp"),
            P(("group", "rep"), "tp"),
            P(("group", "rep"), None, "tp"),
            P(("group", "rep"), None),
            P(("group", "rep")),
            P(("group", "rep")),
            P(("group", "rep")),
            P(("group", "rep"), None),
            P(("group", "rep")),
            P("rep", "tp", None),
            P("rep", None, "tp"),
        ),
        out_specs=P(("group", "rep"), "tp"),
        check_vma=False,
    )
```

```python
import functools
import math

import jax
import jax.numpy as jnp
from jax import lax
from jax.experimental import pallas as pl
from jax.experimental.pallas import tpu as pltpu
from jax.sharding import PartitionSpec as P

HEAD_SIZE = 128
QUERY_GROUP = 8
MCAP = 2
LANES = 128
TOKEN_STEP = 256
HIDDEN = -1e30
SCORE_SCALE = math.log2(math.e) / math.sqrt(HEAD_SIZE)
BIAS_UNIT = float(jnp.bfloat16(1.0 / SCORE_SCALE))
HEADS_STEP = 2
MIB = 1024 * 1024


def whole(array):
    shape = array.shape
    return pl.BlockSpec(shape, lambda *step: (0,) * len(shape))


def smem_spec():
    return pl.BlockSpec(memory_space=pltpu.SMEM)


def params(mebibytes=24):
    return pltpu.CompilerParams(vmem_limit_bytes=mebibytes * MIB)


def cost():
    return pl.CostEstimate(flops=1024, bytes_accessed=1024, transcendentals=0)


def row_to_column(row):
    count = row.shape[1]
    across = lax.broadcasted_iota(jnp.int32, (count, count), 1)
    down = lax.broadcasted_iota(jnp.int32, (count, count), 0)
    return jnp.sum(jnp.where(across == down, row, 0), axis=1, keepdims=True)


def outgoing_kernel(pieces, half_ref, page_ref, target_ref, pool_ref, *refs):
    count_ref, chosen_ref, page_sem, share_sem = refs[-4:]
    out_ref, share_refs, mine_refs = refs[len(pieces)], refs[: len(pieces)], refs[len(pieces) + 1 : -4]
    entry_number = page_ref.shape[0]
    slot_number = out_ref.shape[0]

    def clear(slot, carry):
        chosen_ref[slot] = 0
        count_ref[slot // MCAP] = 0
        return carry

    def place(entry, carry):
        target = target_ref[entry]
        rank = count_ref[target]
        chosen_ref[target * MCAP + rank] = page_ref[entry]
        count_ref[target] = rank + 1
        return carry

    def page_copy(slot):
        return pltpu.make_async_copy(
            pool_ref.at[chosen_ref[slot]], out_ref.at[slot], page_sem.at[slot]
        )

    def send(slot, carry):
        page_copy(slot).start()
        return carry

    def finish(slot, carry):
        page_copy(slot).wait()
        return carry

    shares = []
    for share, cuts in zip(share_refs, pieces):
        for first, last, pack, start in cuts:
            shares.append(
                pltpu.make_async_copy(
                    share.at[half_ref[0], :, pl.ds(first, last - first)],
                    mine_refs[pack].at[:, pl.ds(start, last - first)],
                    share_sem.at[len(shares)],
                )
            )
    lax.fori_loop(0, slot_number, clear, 0)
    lax.fori_loop(0, entry_number, place, 0)
    lax.fori_loop(0, slot_number, send, 0)
    for share in shares:
        share.start()
    lax.fori_loop(0, slot_number, finish, 0)
    for share in shares:
        share.wait()


def outgoing_pages(half, migration_page, migration_target, pool, replicas, shares=(), pieces=(), packs=()):
    slots = replicas * MCAP
    hbm = pl.BlockSpec(memory_space=pltpu.HBM)
    out_shape = [jax.ShapeDtypeStruct((slots,) + pool.shape[1:], pool.dtype)]
    out_shape += [jax.ShapeDtypeStruct(pack, pool.dtype) for pack in packs]
    return pl.pallas_call(
        functools.partial(outgoing_kernel, pieces),
        out_shape=out_shape,
        in_specs=[smem_spec()] * 3 + [hbm] * (1 + len(shares)),
        out_specs=[whole(out) for out in out_shape],
        scratch_shapes=[
            pltpu.SMEM((replicas,), jnp.int32),
            pltpu.SMEM((slots,), jnp.int32),
            pltpu.SemaphoreType.DMA((slots,)),
            pltpu.SemaphoreType.DMA((max(1, sum(len(cuts) for cuts in pieces)),)),
        ],
        compiler_params=params(60),
        cost_estimate=cost(),
        name="outgoing_pages",
    )(half, migration_page, migration_target, pool, *shares)


def token_bias(entries, lengths, first_token, tokens, page_len):
    shape = (tokens, entries.shape[1])
    token = first_token + lax.broadcasted_iota(jnp.int32, shape, 0)
    seen = jnp.zeros(shape, jnp.float32)
    for e in range(entries.shape[0]):
        low = entries[e : e + 1, :] * page_len
        high = low + jnp.clip(lengths - e * page_len, 0, page_len)
        seen = seen + jnp.where((token >= low) & (token < high), 1.0, 0.0)
    return jnp.where(seen > 0.0, jnp.log2(jnp.maximum(seen, 1.0)), HIDDEN)


def identity(rows, on, off):
    across = lax.broadcasted_iota(jnp.int32, (rows, rows), 1)
    down = lax.broadcasted_iota(jnp.int32, (rows, rows), 0)
    return jnp.where(across == down, on, off)


def fill_queries(wide_query_ref, rows):
    ones = identity(rows, BIAS_UNIT, 0.0).astype(jnp.bfloat16)
    for h in range(wide_query_ref.shape[0] // rows):
        wide_query_ref[h * rows : (h + 1) * rows, HEAD_SIZE:] = ones


def fill_keys(wide_key_ref, entries_ref, length_ref, first_token, tokens, page_len):
    for start in range(0, tokens, TOKEN_STEP):
        size = min(TOKEN_STEP, tokens - start)
        bias = token_bias(entries_ref[...], length_ref[...], first_token + start, size, page_len)
        wide_key_ref[start : start + size, HEAD_SIZE:] = bias.astype(jnp.bfloat16)


def score_block(block, wide_query_ref, wide_key_ref, score_ref):
    tokens = score_ref.shape[1]
    top = None
    for start in range(0, tokens, TOKEN_STEP):
        size = min(TOKEN_STEP, tokens - start)
        part = lax.dot_general(
            wide_query_ref[block, :],
            wide_key_ref[start : start + size, :],
            (((1,), (1,)), ((), ())),
            preferred_element_type=jnp.float32,
        )
        score_ref[block, start : start + size] = part
        for lane in range(0, size, LANES):
            piece = part[:, lane : lane + LANES]
            top = piece if top is None else jnp.maximum(top, piece)
    return jnp.max(top, axis=1, keepdims=True)


def weigh_block(block, top, score_ref, weight_ref, wide_value_ref):
    tokens = score_ref.shape[1]
    for start in range(0, tokens, TOKEN_STEP):
        size = min(TOKEN_STEP, tokens - start)
        weights = jnp.exp2((score_ref[block, start : start + size] - top) * SCORE_SCALE)
        weight_ref[block, start : start + size] = weights.astype(jnp.bfloat16)
    return jnp.dot(weight_ref[block, :], wide_value_ref[...], preferred_element_type=jnp.float32)


def load_heads(wide_query_ref, query_ref):
    rows = query_ref.shape[0]
    for h in range(QUERY_GROUP):
        wide_query_ref[h * rows : (h + 1) * rows, :HEAD_SIZE] = query_ref[
            :, h * HEAD_SIZE : (h + 1) * HEAD_SIZE
        ]


def pool_kernel(page_len, query_ref, pool_ref, entries_ref, length_ref, part_ref, stat_ref, *refs):
    wide_query_ref, wide_key_ref, wide_value_ref, score_ref, weight_ref = refs
    rows = query_ref.shape[0]
    tokens = pool_ref.shape[0]

    @pl.when(pl.program_id(0) == 0)
    def _():
        fill_queries(wide_query_ref, rows)
        fill_keys(wide_key_ref, entries_ref, length_ref, 0, tokens, page_len)
        wide_value_ref[:, HEAD_SIZE:] = jnp.ones((tokens, HEAD_SIZE), jnp.bfloat16)

    wide_key_ref[:, :HEAD_SIZE] = pool_ref[:, :HEAD_SIZE]
    wide_value_ref[:, :HEAD_SIZE] = pool_ref[:, HEAD_SIZE:]
    load_heads(wide_query_ref, query_ref)
    lane = lax.broadcasted_iota(jnp.int32, (rows, LANES), 1)
    stats = jnp.zeros((rows, LANES), jnp.float32)
    for h in range(0, QUERY_GROUP, HEADS_STEP):
        block = slice(h * rows, (h + HEADS_STEP) * rows)
        top = score_block(block, wide_query_ref, wide_key_ref, score_ref)
        parts = weigh_block(block, top, score_ref, weight_ref, wide_value_ref)
        total = parts[:, HEAD_SIZE:]
        part_ref[block, :] = (parts[:, :HEAD_SIZE] / total).astype(jnp.bfloat16)
        level = top + jnp.log2(total) * (1.0 / SCORE_SCALE)
        for step in range(HEADS_STEP):
            own = slice(step * rows, (step + 1) * rows)
            stats = jnp.where(lane == h + step, level[own], stats)
    stat_ref[...] = stats


def attend_pool(queries, pool, entries, lengths, page_len):
    rows, width = queries.shape
    tokens = pool.shape[0]
    kv_local = pool.shape[1] // (2 * HEAD_SIZE)
    stacked = QUERY_GROUP * rows
    return pl.pallas_call(
        functools.partial(pool_kernel, page_len),
        grid=(kv_local,),
        out_shape=[
            jax.ShapeDtypeStruct((kv_local * stacked, LANES), jnp.bfloat16),
            jax.ShapeDtypeStruct((rows, kv_local * LANES), jnp.float32),
        ],
        in_specs=[
            pl.BlockSpec((rows, width // kv_local), lambda g: (0, g)),
            pl.BlockSpec((tokens, 2 * HEAD_SIZE), lambda g: (0, g)),
            whole(entries),
            whole(lengths),
        ],
        out_specs=[
            pl.BlockSpec((stacked, LANES), lambda g: (g, 0)),
            pl.BlockSpec((rows, LANES), lambda g: (0, g)),
        ],
        scratch_shapes=[
            pltpu.VMEM((stacked, 2 * HEAD_SIZE), jnp.bfloat16),
            pltpu.VMEM((tokens, 2 * HEAD_SIZE), jnp.bfloat16),
            pltpu.VMEM((tokens, 2 * HEAD_SIZE), jnp.bfloat16),
            pltpu.VMEM((stacked, tokens), jnp.float32),
            pltpu.VMEM((stacked, tokens), jnp.bfloat16),
        ],
        compiler_params=params(),
        cost_estimate=pl.CostEstimate(10**9, 10**7, 10**6),
        name="attend_pool",
    )(queries, pool, entries, lengths)


def finish_kernel(
    page_len,
    first_token,
    place,
    where_ref,
    query_ref,
    part_ref,
    stat_ref,
    arrived_ref,
    fresh_ref,
    entries_ref,
    length_ref,
    target_ref,
    position_ref,
    slot_ref,
    *refs,
):
    out_refs, refs = refs[:-6], refs[-6:]
    wide_query_ref, wide_key_ref, wide_value_ref, score_ref, weight_ref, heads_ref = refs
    rows = query_ref.shape[0]
    g = pl.program_id(0)
    tokens = arrived_ref.shape[0]

    @pl.when(g == 0)
    def _():
        fill_queries(wide_query_ref, rows)
        fill_keys(wide_key_ref, entries_ref, length_ref, first_token, tokens, page_len)
        wide_key_ref[tokens:, HEAD_SIZE:] = identity(rows, 0.0, HIDDEN).astype(jnp.bfloat16)
        wide_value_ref[:, HEAD_SIZE:] = jnp.ones((tokens + rows, HEAD_SIZE), jnp.bfloat16)

    for shelf, first in ((arrived_ref, 0), (fresh_ref, tokens)):
        own = slice(first, first + shelf.shape[0])
        wide_key_ref[own, :HEAD_SIZE] = shelf[:, :HEAD_SIZE]
        wide_value_ref[own, :HEAD_SIZE] = shelf[:, HEAD_SIZE:]
    load_heads(wide_query_ref, query_ref)
    for h in range(0, QUERY_GROUP, HEADS_STEP):
        block = slice(h * rows, (h + HEADS_STEP) * rows)
        level = jnp.concatenate(
            [stat_ref[:, h + step : h + step + 1] for step in range(HEADS_STEP)], axis=0
        )
        top = jnp.maximum(score_block(block, wide_query_ref, wide_key_ref, score_ref), level)
        parts = weigh_block(block, top, score_ref, weight_ref, wide_value_ref)
        pool_weight = jnp.exp2((level - top) * SCORE_SCALE)
        heads = parts[:, :HEAD_SIZE] + pool_weight * part_ref[block, :].astype(jnp.float32)
        heads = (heads / (parts[:, HEAD_SIZE:] + pool_weight)).astype(jnp.bfloat16)
        for step in range(HEADS_STEP):
            heads_ref[g, :, (h + step) * HEAD_SIZE : (h + step + 1) * HEAD_SIZE] = heads[
                step * rows : (step + 1) * rows
            ]

    @pl.when(g == pl.num_programs(0) - 1)
    def _():
        targets = target_ref[...]
        across = lax.broadcasted_iota(jnp.int32, (rows, rows), 1)
        down = lax.broadcasted_iota(jnp.int32, (rows, rows), 0)
        earlier = (row_to_column(targets) == targets) & (down < across)
        rank = jnp.sum(earlier.astype(jnp.int32), axis=0, keepdims=True)
        slots_of = place(targets, where_ref[0]) + rank
        slot_ref[...] = slots_of
        wide = heads_ref.shape[2]
        first = 0
        for out_ref in out_refs:
            slots = out_ref.shape[0]
            slot = first + lax.broadcasted_iota(jnp.int32, (slots, rows), 0)
            pick = slot == slots_of
            label = jnp.sum(jnp.where(pick, position_ref[...], 0), axis=1, keepdims=True)
            pick = pick.astype(jnp.float32).astype(jnp.bfloat16)
            for kv in range(heads_ref.shape[0]):
                out_ref[:, kv * wide : (kv + 1) * wide] = jnp.dot(
                    pick, heads_ref[kv], preferred_element_type=jnp.float32
                ).astype(jnp.bfloat16)
            out_ref[:, heads_ref.shape[0] * wide :] = jnp.broadcast_to(
                label.astype(jnp.float32).astype(jnp.bfloat16), (slots, LANES)
            )
            first += slots


def finish(
    where, queries, found, arrived, fresh, entries, lengths, targets, positions, page_len, first_token, blocks, place
):
    rows, width = queries.shape
    kv_local = arrived.shape[1] // (2 * HEAD_SIZE)
    tokens = arrived.shape[0] + rows
    stacked = QUERY_GROUP * rows
    shelf = lambda array: pl.BlockSpec((array.shape[0], 2 * HEAD_SIZE), lambda g: (0, g))
    small = (entries, lengths, targets, positions)
    out_shape = [jax.ShapeDtypeStruct((1, rows), jnp.int32)]
    out_shape += [jax.ShapeDtypeStruct((block, width + LANES), jnp.bfloat16) for block in blocks]
    return pl.pallas_call(
        functools.partial(finish_kernel, page_len, first_token, place),
        grid=(kv_local,),
        out_shape=out_shape,
        in_specs=[
            smem_spec(),
            pl.BlockSpec((rows, width // kv_local), lambda g: (0, g)),
            pl.BlockSpec((stacked, LANES), lambda g: (g, 0)),
            pl.BlockSpec((rows, LANES), lambda g: (0, g)),
        ]
        + [shelf(array) for array in (arrived, fresh)]
        + [whole(array) for array in small],
        out_specs=[whole(block) for block in out_shape],
        scratch_shapes=[
            pltpu.VMEM((stacked, 2 * HEAD_SIZE), jnp.bfloat16),
            pltpu.VMEM((tokens, 2 * HEAD_SIZE), jnp.bfloat16),
            pltpu.VMEM((tokens, 2 * HEAD_SIZE), jnp.bfloat16),
            pltpu.VMEM((stacked, tokens), jnp.float32),
            pltpu.VMEM((stacked, tokens), jnp.bfloat16),
            pltpu.VMEM((kv_local, rows, width // kv_local), jnp.bfloat16),
        ],
        compiler_params=params(12 + tokens * stacked * 7 // MIB),
        cost_estimate=cost(),
        name="finish",
    )(where, queries, *found, arrived, fresh, *small)


def after_kernel(*refs):
    pass


def after(arrays, *others):
    hbm = pl.BlockSpec(memory_space=pl.ANY)
    return pl.pallas_call(
        after_kernel,
        out_shape=[jax.ShapeDtypeStruct(array.shape, array.dtype) for array in arrays],
        in_specs=[hbm] * (len(arrays) + len(others)),
        out_specs=[hbm] * len(arrays),
        input_output_aliases={i: i for i in range(len(arrays))},
        compiler_params=params(1),
        cost_estimate=cost(),
        name="after",
    )(*arrays, *others)


def down_kernel(half_ref, *refs):
    block_refs, (own_ref, first_ref, second_ref, out_ref, rows_ref) = refs[:-5], refs[-5:]
    cap = out_ref.shape[0] // 8
    width = own_ref.shape[1]
    for b, block in enumerate(block_refs):
        rows_ref[b * cap : (b + 1) * cap, :] = block[:cap, :]
        rows_ref[(b + 4) * cap : (b + 5) * cap, :] = block[cap:, :]
    swapped = half_ref[0] == 1
    zero = jnp.where(swapped, second_ref[...], first_ref[...])
    one = jnp.where(swapped, first_ref[...], second_ref[...])
    lane = lax.broadcasted_iota(jnp.int32, (1, out_ref.shape[1]), 1)
    adapter = jnp.where(lane < out_ref.shape[1] // 2, 0.0, 1.0)
    for start, weights in ((0, own_ref[...]), (4 * cap, jnp.concatenate([zero, one], axis=0))):
        part = slice(start, start + 4 * cap)
        product = lax.dot_general(
            rows_ref[part, :width],
            weights,
            (((1,), (1,)), ((), ())),
            preferred_element_type=jnp.float32,
        )
        label = rows_ref[part, width:].astype(jnp.float32)
        out_ref[part, :] = jnp.where(label == adapter, product, 0.0)


def low_products(half, blocks, own, first, second):
    rows = sum(block.shape[0] for block in blocks)
    inputs = (*blocks, own, first, second)
    out_shape = jax.ShapeDtypeStruct((rows, own.shape[0]), jnp.float32)
    return pl.pallas_call(
        down_kernel,
        grid=(1,),
        out_shape=out_shape,
        in_specs=[smem_spec()]
        + [whole(array) for array in (*blocks, own)]
        + [pl.BlockSpec((first.shape[0], own.shape[1]), lambda *step: (0, 0))] * 2,
        out_specs=whole(out_shape),
        scratch_shapes=[pltpu.VMEM((rows, blocks[0].shape[1]), jnp.bfloat16)],
        compiler_params=params(),
        cost_estimate=cost(),
        name="low_products",
    )(half, *inputs)


def lift(low_refs, weights, out_refs):
    low = (low_refs[0][...] + low_refs[1][...]).astype(jnp.bfloat16)
    lifted = jnp.dot(low, weights, preferred_element_type=jnp.float32).astype(jnp.bfloat16)
    cap = out_refs[0].shape[0]
    for b, out_ref in enumerate(out_refs):
        out_ref[...] = lifted[b * cap : (b + 1) * cap]


def lift_own_kernel(mine_ref, other_ref, own_ref, *out_refs):
    lift((mine_ref, other_ref), own_ref[...], out_refs)


def lift_own(mine, other, weights):
    rows, rank = mine.shape
    width = weights.shape[1]
    step = width
    low = pl.BlockSpec((rows // 2, rank), lambda j: (0, 0))
    out = jax.ShapeDtypeStruct((rows // 8, width), jnp.bfloat16)
    return pl.pallas_call(
        lift_own_kernel,
        grid=(width // step,),
        out_shape=(out,) * 4,
        in_specs=[low, low, pl.BlockSpec((rank, step), lambda j: (0, j))],
        out_specs=[pl.BlockSpec((rows // 8, step), lambda j: (0, j))] * 4,
        compiler_params=params(),
        cost_estimate=cost(),
        name="lift_own",
    )(mine, other, weights)


def lift_far_kernel(half_ref, mine_ref, other_ref, *refs):
    number = (len(refs) - 4) // 2
    first_refs, second_refs, out_refs = refs[:number], refs[number : 2 * number], refs[2 * number :]
    low = (mine_ref[...] + other_ref[...]).astype(jnp.bfloat16)
    swapped = half_ref[0] == 1
    cap = out_refs[0].shape[0]
    place = 0
    for first_ref, second_ref in zip(first_refs, second_refs):
        columns = slice(place, place + first_ref.shape[1])
        zero = jnp.where(swapped, second_ref[...], first_ref[...])
        one = jnp.where(swapped, first_ref[...], second_ref[...])
        lifted = jnp.dot(
            low, jnp.concatenate([zero, one], axis=0), preferred_element_type=jnp.float32
        ).astype(jnp.bfloat16)
        for b, out_ref in enumerate(out_refs):
            out_ref[:, columns] = lifted[b * cap : (b + 1) * cap]
        place = columns.stop


def lift_far(half, mine, other, first, second):
    rows, rank = mine.shape
    width = sum(piece.shape[1] for piece in first)
    low = pl.BlockSpec((rows // 2, rank), lambda j: (1, 0))
    out = jax.ShapeDtypeStruct((rows // 8, width), jnp.bfloat16)
    return pl.pallas_call(
        lift_far_kernel,
        grid=(1,),
        out_shape=(out,) * 4,
        in_specs=[smem_spec(), low, low] + [whole(piece) for piece in (*first, *second)],
        out_specs=[whole(out)] * 4,
        compiler_params=params(),
        cost_estimate=cost(),
        name="lift_far",
    )(half, mine, other, *first, *second)


def gather_rows_kernel(slot_ref, *refs):
    out_ref = refs[-1]
    rows = out_ref.shape[0]
    stacked = jnp.concatenate([ref[...] for ref in refs[:-1]], axis=0)
    slot = lax.broadcasted_iota(jnp.int32, (rows, stacked.shape[0]), 1)
    pick = (slot == row_to_column(slot_ref[...])).astype(jnp.float32).astype(jnp.bfloat16)
    out_ref[...] = jnp.dot(pick, stacked, preferred_element_type=jnp.float32).astype(jnp.bfloat16)


def gather_rows(slots, blocks):
    rows = slots.shape[1]
    width = blocks[0].shape[1]
    step = 4096
    return pl.pallas_call(
        gather_rows_kernel,
        grid=(width // step,),
        out_shape=jax.ShapeDtypeStruct((rows, width), jnp.bfloat16),
        in_specs=[pl.BlockSpec(slots.shape, lambda j: (0, 0))]
        + [pl.BlockSpec((block.shape[0], step), lambda j: (0, j)) for block in blocks],
        out_specs=pl.BlockSpec((rows, step), lambda j: (0, j)),
        compiler_params=params(),
        cost_estimate=cost(),
        name="gather_rows",
    )(slots, *blocks)


def along(array, group_bit, replica_bits):
    groups, replicas = lax.axis_size("group"), lax.axis_size("rep")
    pairs = [
        (g * replicas + r, (g ^ group_bit) * replicas + (r ^ replica_bits))
        for g in range(groups)
        for r in range(replicas)
    ]
    return lax.ppermute(array, ("group", "rep"), pairs)


def shared_local(
    queries,
    current_key_value,
    key_value_pool,
    request_page_entries,
    context_length,
    migration_page,
    migration_target,
    adapter_replica,
    adapter_position,
    adapter_down_weight,
    adapter_up_weight,
):
    rows, width = queries.shape
    replicas = lax.axis_size("rep")
    cap = 2 * rows // replicas
    group = lax.axis_index("group")
    half = group.reshape(1).astype(jnp.int32)
    where = jnp.stack([lax.axis_index("rep"), group]).astype(jnp.int32)
    targets = adapter_replica.reshape(1, -1)
    down_rows = jnp.swapaxes(adapter_down_weight, 1, 2)
    down = down_rows.reshape(-1, width)
    up = adapter_up_weight.reshape(-1, adapter_up_weight.shape[2])
    entries = request_page_entries.T
    lengths = context_length.reshape(1, -1)
    positions = adapter_position.reshape(1, -1)
    pages, page_len, features = key_value_pool.shape
    pool = key_value_pool.reshape(pages * page_len, features)

    columns = up.shape[1]
    early = columns // 8 * 5
    rank = up.shape[0] // 2
    outgoing, *packs = outgoing_pages(
        half,
        migration_page,
        migration_target,
        key_value_pool,
        replicas,
        (down_rows, adapter_up_weight),
        (((0, width, 0, 0),), ((0, early, 1, 0), (early, columns, 2, 0))),
        ((rank, width), (rank, early), (rank, columns - early)),
    )
    arrived = lax.all_to_all(outgoing, "rep", split_axis=0, concat_axis=0, tiled=True)
    found = attend_pool(queries, pool, entries, lengths, page_len)
    first = [along(*after(packs[:1], arrived, found[1]), 0, 6), along(packs[1], 0, 6)]

    def place(targets, replica):
        apart = jnp.bitwise_xor(targets, replica)
        far = jnp.right_shift(apart, 2)
        return (2 * jnp.bitwise_xor(jnp.bitwise_and(apart, 3), 2 * far) + far) * cap

    slots, here, *outbound = finish(
        where,
        queries,
        found,
        arrived.reshape(-1, features),
        current_key_value,
        entries,
        lengths,
        targets,
        positions,
        page_len,
        pages * page_len,
        (2 * cap,) * 4,
        place,
    )
    blocks = [along(block, 0, 3 - b) for b, block in enumerate(outbound[::-1])]
    blocks = [here] + blocks[::-1]
    first.append(along(*after([packs[2]], blocks[3]), 0, 6))
    second = [along(*after([first[0]], slots), 1, 0), along(*after([first[1]], blocks[1]), 1, 0)]
    mine = low_products(half, blocks, down, first[0], second[0])
    other = lax.ppermute(mine, "tp", [(0, 1), (1, 0)])
    second.append(along(*after([first[2]], other), 1, 0))
    own = lift_own(mine, other, up)
    own = [block if b == 0 else along(block, 0, b) for b, block in enumerate(own)]
    far = lift_far(half, mine, other, first[1:], second[1:])
    far = [block if b == 0 else along(block, 0, b) for b, block in enumerate(far)]
    return gather_rows(slots, [block for pair in zip(own, far) for block in pair])


def local(
    queries,
    current_key_value,
    key_value_pool,
    request_page_entries,
    context_length,
    migration_page,
    migration_target,
    adapter_replica,
    adapter_position,
    adapter_down_weight,
    adapter_up_weight,
):
    replicas = lax.axis_size("rep")
    if replicas == 8 and lax.axis_size("group") == 2 and adapter_down_weight.shape[0] == 2:
        return shared_local(
            queries,
            current_key_value,
            key_value_pool,
            request_page_entries,
            context_length,
            migration_page,
            migration_target,
            adapter_replica,
            adapter_position,
            adapter_down_weight,
            adapter_up_weight,
        )
    rows, width = queries.shape
    adapter_number = adapter_down_weight.shape[0]
    slot_cap = max(2, (2 * rows + replicas - 1) // replicas)
    entries = request_page_entries.T
    lengths = context_length.reshape(1, -1)
    pages, page_len, features = key_value_pool.shape
    pool = key_value_pool.reshape(pages * page_len, features)
    where = jnp.stack([lax.axis_index("rep"), lax.axis_index("group")]).astype(jnp.int32)
    (outgoing,) = outgoing_pages(where, migration_page, migration_target, key_value_pool, replicas)
    arrived = lax.all_to_all(outgoing, "rep", split_axis=0, concat_axis=0, tiled=True)
    found = attend_pool(queries, pool, entries, lengths, page_len)
    slots, outbound = finish(
        where,
        queries,
        found,
        arrived.reshape(-1, features),
        current_key_value,
        entries,
        lengths,
        adapter_replica.reshape(1, -1),
        adapter_position.reshape(1, -1),
        page_len,
        pages * page_len,
        (replicas * slot_cap,),
        lambda targets, replica: targets * slot_cap,
    )
    outbound = outbound.reshape(replicas, slot_cap, -1)
    activations = lax.all_to_all(outbound, "rep", split_axis=0, concat_axis=0, tiled=True)
    shape_in = activations.shape
    flat_output = activations.reshape(-1, shape_in[2])
    selector = (
        flat_output[:, width : width + 1].astype(jnp.int32)
        == jnp.arange(adapter_number, dtype=jnp.int32)[None, :]
    )
    reduced_rank_total = jnp.einsum(
        "oh,pht->opt", flat_output[:, :width], adapter_down_weight, preferred_element_type=jnp.float32
    )
    partial_low = jnp.sum(jnp.where(selector[:, :, None], reduced_rank_total, 0.0), axis=1)
    low_rank = lax.psum(partial_low, "tp").astype(jnp.bfloat16)
    broadcast_result = jnp.where(
        selector[:, :, None], low_rank[:, None, :], jnp.zeros((), jnp.bfloat16)
    )
    broadcast_result = broadcast_result.reshape(flat_output.shape[0], -1)
    lifted = jnp.dot(
        broadcast_result,
        adapter_up_weight.reshape(-1, adapter_up_weight.shape[2]),
        preferred_element_type=jnp.float32,
    )
    lifted = lifted.astype(jnp.bfloat16).reshape(shape_in[0], shape_in[1], -1)
    returned = lax.all_to_all(lifted, "rep", split_axis=0, concat_axis=0, tiled=True)
    route_mask = (
        jnp.arange(replicas * slot_cap, dtype=jnp.int32)[:, None] == slots
    ).astype(jnp.bfloat16)
    delta = jnp.einsum(
        "sr,sd->rd",
        route_mask,
        returned.reshape(replicas * slot_cap, -1),
        preferred_element_type=jnp.float32,
    )
    return delta.astype(jnp.bfloat16)


def solution(mesh):
    return jax.shard_map(
        local,
        mesh=mesh,
        in_specs=(
            P(("group", "rep"), "tp"),
            P(("group", "rep"), "tp"),
            P(("group", "rep"), None, "tp"),
            P(("group", "rep"), None),
            P(("group", "rep")),
            P(("group", "rep")),
            P(("group", "rep")),
            P(("group", "rep"), None),
            P(("group", "rep")),
            P("rep", "tp", None),
            P("rep", None, "tp"),
        ),
        out_specs=P(("group", "rep"), "tp"),
        check_vma=False,
    )
```

```python
import functools
import math

import jax
import jax.numpy as jnp
from jax import lax
from jax.experimental import pallas as pl
from jax.experimental.pallas import tpu as pltpu
from jax.sharding import PartitionSpec as P

HEAD_SIZE = 128
QUERY_GROUP = 8
MCAP = 2
LANES = 128
TOKEN_STEP = 256
HIDDEN = -1e30
SCORE_SCALE = math.log2(math.e) / math.sqrt(HEAD_SIZE)
BIAS_UNIT = float(jnp.bfloat16(1.0 / SCORE_SCALE))
HEADS_STEP = 2
MIB = 1024 * 1024


def whole(array):
    shape = array.shape
    return pl.BlockSpec(shape, lambda *step: (0,) * len(shape))


def smem_spec():
    return pl.BlockSpec(memory_space=pltpu.SMEM)


def params(mebibytes=24):
    return pltpu.CompilerParams(vmem_limit_bytes=mebibytes * MIB)


def cost():
    return pl.CostEstimate(flops=1024, bytes_accessed=1024, transcendentals=0)


def row_to_column(row):
    count = row.shape[1]
    across = lax.broadcasted_iota(jnp.int32, (count, count), 1)
    down = lax.broadcasted_iota(jnp.int32, (count, count), 0)
    return jnp.sum(jnp.where(across == down, row, 0), axis=1, keepdims=True)


def outgoing_kernel(pieces, half_ref, page_ref, target_ref, pool_ref, *refs):
    count_ref, chosen_ref, page_sem, share_sem = refs[-4:]
    out_ref, share_refs, mine_refs = refs[len(pieces)], refs[: len(pieces)], refs[len(pieces) + 1 : -4]
    entry_number = page_ref.shape[0]
    slot_number = out_ref.shape[0]

    def clear(slot, carry):
        chosen_ref[slot] = 0
        count_ref[slot // MCAP] = 0
        return carry

    def place(entry, carry):
        target = target_ref[entry]
        rank = count_ref[target]
        chosen_ref[target * MCAP + rank] = page_ref[entry]
        count_ref[target] = rank + 1
        return carry

    def page_copy(slot):
        return pltpu.make_async_copy(
            pool_ref.at[chosen_ref[slot]], out_ref.at[slot], page_sem.at[slot]
        )

    def send(slot, carry):
        page_copy(slot).start()
        return carry

    def finish(slot, carry):
        page_copy(slot).wait()
        return carry

    shares = []
    for share, cuts in zip(share_refs, pieces):
        for first, last, pack, start in cuts:
            shares.append(
                pltpu.make_async_copy(
                    share.at[half_ref[0], :, pl.ds(first, last - first)],
                    mine_refs[pack].at[:, pl.ds(start, last - first)],
                    share_sem.at[len(shares)],
                )
            )
    for share in shares:
        share.start()
    unroll = slot_number <= 16
    lax.fori_loop(0, slot_number, clear, 0, unroll=unroll)
    lax.fori_loop(0, entry_number, place, 0, unroll=unroll)
    lax.fori_loop(0, slot_number, send, 0, unroll=unroll)
    lax.fori_loop(0, slot_number, finish, 0, unroll=unroll)
    for share in shares:
        share.wait()


def outgoing_pages(half, migration_page, migration_target, pool, replicas, shares=(), pieces=(), packs=()):
    slots = replicas * MCAP
    hbm = pl.BlockSpec(memory_space=pltpu.HBM)
    out_shape = [jax.ShapeDtypeStruct((slots,) + pool.shape[1:], pool.dtype)]
    out_shape += [jax.ShapeDtypeStruct(pack, pool.dtype) for pack in packs]
    return pl.pallas_call(
        functools.partial(outgoing_kernel, pieces),
        out_shape=out_shape,
        in_specs=[smem_spec()] * 3 + [hbm] * (1 + len(shares)),
        out_specs=[whole(out) for out in out_shape],
        scratch_shapes=[
            pltpu.SMEM((replicas,), jnp.int32),
            pltpu.SMEM((slots,), jnp.int32),
            pltpu.SemaphoreType.DMA((slots,)),
            pltpu.SemaphoreType.DMA((max(1, sum(len(cuts) for cuts in pieces)),)),
        ],
        compiler_params=params(60),
        cost_estimate=cost(),
        name="outgoing_pages",
    )(half, migration_page, migration_target, pool, *shares)


def token_bias(entries, lengths, first_token, tokens, page_len):
    shape = (tokens, entries.shape[1])
    token = first_token + lax.broadcasted_iota(jnp.int32, shape, 0)
    seen = jnp.zeros(shape, jnp.float32)
    for e in range(entries.shape[0]):
        low = entries[e : e + 1, :] * page_len
        high = low + jnp.clip(lengths - e * page_len, 0, page_len)
        seen = seen + jnp.where((token >= low) & (token < high), 1.0, 0.0)
    return jnp.where(seen > 0.0, jnp.log2(jnp.maximum(seen, 1.0)), HIDDEN)


def identity(rows, on, off):
    across = lax.broadcasted_iota(jnp.int32, (rows, rows), 1)
    down = lax.broadcasted_iota(jnp.int32, (rows, rows), 0)
    return jnp.where(across == down, on, off)


def fill_queries(wide_query_ref, rows):
    ones = identity(rows, BIAS_UNIT, 0.0).astype(jnp.bfloat16)
    for h in range(wide_query_ref.shape[0] // rows):
        wide_query_ref[h * rows : (h + 1) * rows, HEAD_SIZE:] = ones


def fill_keys(wide_key_ref, entries_ref, length_ref, first_token, tokens, page_len):
    for start in range(0, tokens, TOKEN_STEP):
        size = min(TOKEN_STEP, tokens - start)
        bias = token_bias(entries_ref[...], length_ref[...], first_token + start, size, page_len)
        wide_key_ref[start : start + size, HEAD_SIZE:] = bias.astype(jnp.bfloat16)


def score_block(block, wide_query_ref, wide_key_ref, score_ref):
    tokens = score_ref.shape[1]
    top = None
    for start in range(0, tokens, TOKEN_STEP):
        size = min(TOKEN_STEP, tokens - start)
        part = lax.dot_general(
            wide_query_ref[block, :],
            wide_key_ref[start : start + size, :],
            (((1,), (1,)), ((), ())),
            preferred_element_type=jnp.float32,
        )
        score_ref[block, start : start + size] = part
        for lane in range(0, size, LANES):
            piece = part[:, lane : lane + LANES]
            top = piece if top is None else jnp.maximum(top, piece)
    return jnp.max(top, axis=1, keepdims=True)


def weigh_block(block, top, score_ref, weight_ref, wide_value_ref):
    tokens = score_ref.shape[1]
    for start in range(0, tokens, TOKEN_STEP):
        size = min(TOKEN_STEP, tokens - start)
        weights = jnp.exp2((score_ref[block, start : start + size] - top) * SCORE_SCALE)
        weight_ref[block, start : start + size] = weights.astype(jnp.bfloat16)
    return jnp.dot(weight_ref[block, :], wide_value_ref[...], preferred_element_type=jnp.float32)


def load_heads(wide_query_ref, query_ref):
    rows = query_ref.shape[0]
    for h in range(QUERY_GROUP):
        wide_query_ref[h * rows : (h + 1) * rows, :HEAD_SIZE] = query_ref[
            :, h * HEAD_SIZE : (h + 1) * HEAD_SIZE
        ]


def pool_kernel(page_len, query_ref, pool_ref, entries_ref, length_ref, part_ref, stat_ref, *refs):
    wide_query_ref, wide_key_ref, wide_value_ref, score_ref, weight_ref = refs
    rows = query_ref.shape[0]
    tokens = pool_ref.shape[0]

    @pl.when(pl.program_id(0) == 0)
    def _():
        fill_queries(wide_query_ref, rows)
        fill_keys(wide_key_ref, entries_ref, length_ref, 0, tokens, page_len)
        wide_value_ref[:, HEAD_SIZE:] = jnp.ones((tokens, HEAD_SIZE), jnp.bfloat16)

    wide_key_ref[:, :HEAD_SIZE] = pool_ref[:, :HEAD_SIZE]
    wide_value_ref[:, :HEAD_SIZE] = pool_ref[:, HEAD_SIZE:]
    load_heads(wide_query_ref, query_ref)
    lane = lax.broadcasted_iota(jnp.int32, (rows, LANES), 1)
    stats = jnp.zeros((rows, LANES), jnp.float32)
    for h in range(0, QUERY_GROUP, HEADS_STEP):
        block = slice(h * rows, (h + HEADS_STEP) * rows)
        top = score_block(block, wide_query_ref, wide_key_ref, score_ref)
        parts = weigh_block(block, top, score_ref, weight_ref, wide_value_ref)
        total = parts[:, HEAD_SIZE:]
        part_ref[block, :] = (parts[:, :HEAD_SIZE] / total).astype(jnp.bfloat16)
        level = top + jnp.log2(total) * (1.0 / SCORE_SCALE)
        for step in range(HEADS_STEP):
            own = slice(step * rows, (step + 1) * rows)
            stats = jnp.where(lane == h + step, level[own], stats)
    stat_ref[...] = stats


def attend_pool(queries, pool, entries, lengths, page_len):
    rows, width = queries.shape
    tokens = pool.shape[0]
    kv_local = pool.shape[1] // (2 * HEAD_SIZE)
    stacked = QUERY_GROUP * rows
    return pl.pallas_call(
        functools.partial(pool_kernel, page_len),
        grid=(kv_local,),
        out_shape=[
            jax.ShapeDtypeStruct((kv_local * stacked, LANES), jnp.bfloat16),
            jax.ShapeDtypeStruct((rows, kv_local * LANES), jnp.float32),
        ],
        in_specs=[
            pl.BlockSpec((rows, width // kv_local), lambda g: (0, g)),
            pl.BlockSpec((tokens, 2 * HEAD_SIZE), lambda g: (0, g)),
            whole(entries),
            whole(lengths),
        ],
        out_specs=[
            pl.BlockSpec((stacked, LANES), lambda g: (g, 0)),
            pl.BlockSpec((rows, LANES), lambda g: (0, g)),
        ],
        scratch_shapes=[
            pltpu.VMEM((stacked, 2 * HEAD_SIZE), jnp.bfloat16),
            pltpu.VMEM((tokens, 2 * HEAD_SIZE), jnp.bfloat16),
            pltpu.VMEM((tokens, 2 * HEAD_SIZE), jnp.bfloat16),
            pltpu.VMEM((stacked, tokens), jnp.float32),
            pltpu.VMEM((stacked, tokens), jnp.bfloat16),
        ],
        compiler_params=params(),
        cost_estimate=pl.CostEstimate(10**9, 10**7, 10**6),
        name="attend_pool",
    )(queries, pool, entries, lengths)


def finish_kernel(
    page_len,
    first_token,
    place,
    where_ref,
    query_ref,
    part_ref,
    stat_ref,
    arrived_ref,
    fresh_ref,
    entries_ref,
    length_ref,
    target_ref,
    position_ref,
    slot_ref,
    *refs,
):
    out_refs, refs = refs[:-6], refs[-6:]
    wide_query_ref, wide_key_ref, wide_value_ref, score_ref, weight_ref, heads_ref = refs
    rows = query_ref.shape[0]
    g = pl.program_id(0)
    tokens = arrived_ref.shape[0]

    @pl.when(g == 0)
    def _():
        fill_queries(wide_query_ref, rows)
        fill_keys(wide_key_ref, entries_ref, length_ref, first_token, tokens, page_len)
        wide_key_ref[tokens:, HEAD_SIZE:] = identity(rows, 0.0, HIDDEN).astype(jnp.bfloat16)
        wide_value_ref[:, HEAD_SIZE:] = jnp.ones((tokens + rows, HEAD_SIZE), jnp.bfloat16)

    for shelf, first in ((arrived_ref, 0), (fresh_ref, tokens)):
        own = slice(first, first + shelf.shape[0])
        wide_key_ref[own, :HEAD_SIZE] = shelf[:, :HEAD_SIZE]
        wide_value_ref[own, :HEAD_SIZE] = shelf[:, HEAD_SIZE:]
    load_heads(wide_query_ref, query_ref)
    for h in range(0, QUERY_GROUP, HEADS_STEP):
        block = slice(h * rows, (h + HEADS_STEP) * rows)
        level = jnp.concatenate(
            [stat_ref[:, h + step : h + step + 1] for step in range(HEADS_STEP)], axis=0
        )
        top = jnp.maximum(score_block(block, wide_query_ref, wide_key_ref, score_ref), level)
        parts = weigh_block(block, top, score_ref, weight_ref, wide_value_ref)
        pool_weight = jnp.exp2((level - top) * SCORE_SCALE)
        heads = parts[:, :HEAD_SIZE] + pool_weight * part_ref[block, :].astype(jnp.float32)
        heads = (heads / (parts[:, HEAD_SIZE:] + pool_weight)).astype(jnp.bfloat16)
        for step in range(HEADS_STEP):
            heads_ref[g, :, (h + step) * HEAD_SIZE : (h + step + 1) * HEAD_SIZE] = heads[
                step * rows : (step + 1) * rows
            ]

    @pl.when(g == pl.num_programs(0) - 1)
    def _():
        targets = target_ref[...]
        across = lax.broadcasted_iota(jnp.int32, (rows, rows), 1)
        down = lax.broadcasted_iota(jnp.int32, (rows, rows), 0)
        earlier = (row_to_column(targets) == targets) & (down < across)
        rank = jnp.sum(earlier.astype(jnp.int32), axis=0, keepdims=True)
        slots_of = place(targets, where_ref[0]) + rank
        slot_ref[...] = slots_of
        wide = heads_ref.shape[2]
        first = 0
        for out_ref in out_refs:
            slots = out_ref.shape[0]
            slot = first + lax.broadcasted_iota(jnp.int32, (slots, rows), 0)
            pick = slot == slots_of
            label = jnp.sum(jnp.where(pick, position_ref[...], 0), axis=1, keepdims=True)
            pick = pick.astype(jnp.float32).astype(jnp.bfloat16)
            for kv in range(heads_ref.shape[0]):
                out_ref[:, kv * wide : (kv + 1) * wide] = jnp.dot(
                    pick, heads_ref[kv], preferred_element_type=jnp.float32
                ).astype(jnp.bfloat16)
            out_ref[:, heads_ref.shape[0] * wide :] = jnp.broadcast_to(
                label.astype(jnp.float32).astype(jnp.bfloat16), (slots, LANES)
            )
            first += slots


def finish(
    where, queries, found, arrived, fresh, entries, lengths, targets, positions, page_len, first_token, blocks, place
):
    rows, width = queries.shape
    kv_local = arrived.shape[1] // (2 * HEAD_SIZE)
    tokens = arrived.shape[0] + rows
    stacked = QUERY_GROUP * rows
    shelf = lambda array: pl.BlockSpec((array.shape[0], 2 * HEAD_SIZE), lambda g: (0, g))
    small = (entries, lengths, targets, positions)
    out_shape = [jax.ShapeDtypeStruct((1, rows), jnp.int32)]
    out_shape += [jax.ShapeDtypeStruct((block, width + LANES), jnp.bfloat16) for block in blocks]
    return pl.pallas_call(
        functools.partial(finish_kernel, page_len, first_token, place),
        grid=(kv_local,),
        out_shape=out_shape,
        in_specs=[
            smem_spec(),
            pl.BlockSpec((rows, width // kv_local), lambda g: (0, g)),
            pl.BlockSpec((stacked, LANES), lambda g: (g, 0)),
            pl.BlockSpec((rows, LANES), lambda g: (0, g)),
        ]
        + [shelf(array) for array in (arrived, fresh)]
        + [whole(array) for array in small],
        out_specs=[whole(block) for block in out_shape],
        scratch_shapes=[
            pltpu.VMEM((stacked, 2 * HEAD_SIZE), jnp.bfloat16),
            pltpu.VMEM((tokens, 2 * HEAD_SIZE), jnp.bfloat16),
            pltpu.VMEM((tokens, 2 * HEAD_SIZE), jnp.bfloat16),
            pltpu.VMEM((stacked, tokens), jnp.float32),
            pltpu.VMEM((stacked, tokens), jnp.bfloat16),
            pltpu.VMEM((kv_local, rows, width // kv_local), jnp.bfloat16),
        ],
        compiler_params=params(12 + tokens * stacked * 7 // MIB),
        cost_estimate=cost(),
        name="finish",
    )(where, queries, *found, arrived, fresh, *small)


def after_kernel(*refs):
    pass


def after(arrays, *others):
    hbm = pl.BlockSpec(memory_space=pl.ANY)
    return pl.pallas_call(
        after_kernel,
        out_shape=[jax.ShapeDtypeStruct(array.shape, array.dtype) for array in arrays],
        in_specs=[hbm] * (len(arrays) + len(others)),
        out_specs=[hbm] * len(arrays),
        input_output_aliases={i: i for i in range(len(arrays))},
        compiler_params=params(1),
        cost_estimate=cost(),
        name="after",
    )(*arrays, *others)


def down_kernel(half_ref, *refs):
    block_refs, (own_ref, first_ref, second_ref, out_ref, rows_ref) = refs[:-5], refs[-5:]
    cap = out_ref.shape[0] // 8
    width = own_ref.shape[1]
    for b, block in enumerate(block_refs):
        rows_ref[b * cap : (b + 1) * cap, :] = block[:cap, :]
        rows_ref[(b + 4) * cap : (b + 5) * cap, :] = block[cap:, :]
    swapped = half_ref[0] == 1
    zero = jnp.where(swapped, second_ref[...], first_ref[...])
    one = jnp.where(swapped, first_ref[...], second_ref[...])
    lane = lax.broadcasted_iota(jnp.int32, (1, out_ref.shape[1]), 1)
    adapter = jnp.where(lane < out_ref.shape[1] // 2, 0.0, 1.0)
    for start, weights in ((0, own_ref[...]), (4 * cap, jnp.concatenate([zero, one], axis=0))):
        part = slice(start, start + 4 * cap)
        product = lax.dot_general(
            rows_ref[part, :width],
            weights,
            (((1,), (1,)), ((), ())),
            preferred_element_type=jnp.float32,
        )
        label = rows_ref[part, width:].astype(jnp.float32)
        out_ref[part, :] = jnp.where(label == adapter, product, 0.0)


def low_products(half, blocks, own, first, second):
    rows = sum(block.shape[0] for block in blocks)
    inputs = (*blocks, own, first, second)
    out_shape = jax.ShapeDtypeStruct((rows, own.shape[0]), jnp.float32)
    return pl.pallas_call(
        down_kernel,
        grid=(1,),
        out_shape=out_shape,
        in_specs=[smem_spec()]
        + [whole(array) for array in (*blocks, own)]
        + [pl.BlockSpec((first.shape[0], own.shape[1]), lambda *step: (0, 0))] * 2,
        out_specs=whole(out_shape),
        scratch_shapes=[pltpu.VMEM((rows, blocks[0].shape[1]), jnp.bfloat16)],
        compiler_params=params(),
        cost_estimate=cost(),
        name="low_products",
    )(half, *inputs)


def lift(low_refs, weights, out_refs):
    low = (low_refs[0][...] + low_refs[1][...]).astype(jnp.bfloat16)
    lifted = jnp.dot(low, weights, preferred_element_type=jnp.float32).astype(jnp.bfloat16)
    cap = out_refs[0].shape[0]
    for b, out_ref in enumerate(out_refs):
        out_ref[...] = lifted[b * cap : (b + 1) * cap]


def lift_own_kernel(mine_ref, other_ref, own_ref, *out_refs):
    lift((mine_ref, other_ref), own_ref[...], out_refs)


def lift_own(mine, other, weights):
    rows, rank = mine.shape
    width = weights.shape[1]
    step = width
    low = pl.BlockSpec((rows // 2, rank), lambda j: (0, 0))
    out = jax.ShapeDtypeStruct((rows // 8, width), jnp.bfloat16)
    return pl.pallas_call(
        lift_own_kernel,
        grid=(width // step,),
        out_shape=(out,) * 4,
        in_specs=[low, low, pl.BlockSpec((rank, step), lambda j: (0, j))],
        out_specs=[pl.BlockSpec((rows // 8, step), lambda j: (0, j))] * 4,
        compiler_params=params(),
        cost_estimate=cost(),
        name="lift_own",
    )(mine, other, weights)


def lift_far_kernel(half_ref, mine_ref, other_ref, *refs):
    number = (len(refs) - 4) // 2
    first_refs, second_refs, out_refs = refs[:number], refs[number : 2 * number], refs[2 * number :]
    low = (mine_ref[...] + other_ref[...]).astype(jnp.bfloat16)
    swapped = half_ref[0] == 1
    cap = out_refs[0].shape[0]
    place = 0
    for first_ref, second_ref in zip(first_refs, second_refs):
        columns = slice(place, place + first_ref.shape[1])
        zero = jnp.where(swapped, second_ref[...], first_ref[...])
        one = jnp.where(swapped, first_ref[...], second_ref[...])
        lifted = jnp.dot(
            low, jnp.concatenate([zero, one], axis=0), preferred_element_type=jnp.float32
        ).astype(jnp.bfloat16)
        for b, out_ref in enumerate(out_refs):
            out_ref[:, columns] = lifted[b * cap : (b + 1) * cap]
        place = columns.stop


def lift_far(half, mine, other, first, second):
    rows, rank = mine.shape
    width = sum(piece.shape[1] for piece in first)
    low = pl.BlockSpec((rows // 2, rank), lambda j: (1, 0))
    out = jax.ShapeDtypeStruct((rows // 8, width), jnp.bfloat16)
    return pl.pallas_call(
        lift_far_kernel,
        grid=(1,),
        out_shape=(out,) * 4,
        in_specs=[smem_spec(), low, low] + [whole(piece) for piece in (*first, *second)],
        out_specs=[whole(out)] * 4,
        compiler_params=params(),
        cost_estimate=cost(),
        name="lift_far",
    )(half, mine, other, *first, *second)


def gather_rows_kernel(slot_ref, *refs):
    out_ref = refs[-1]
    rows = out_ref.shape[0]
    stacked = jnp.concatenate([ref[...] for ref in refs[:-1]], axis=0)
    slot = lax.broadcasted_iota(jnp.int32, (rows, stacked.shape[0]), 1)
    pick = (slot == row_to_column(slot_ref[...])).astype(jnp.float32).astype(jnp.bfloat16)
    out_ref[...] = jnp.dot(pick, stacked, preferred_element_type=jnp.float32).astype(jnp.bfloat16)


def gather_rows(slots, blocks):
    rows = slots.shape[1]
    width = blocks[0].shape[1]
    step = 4096
    return pl.pallas_call(
        gather_rows_kernel,
        grid=(width // step,),
        out_shape=jax.ShapeDtypeStruct((rows, width), jnp.bfloat16),
        in_specs=[pl.BlockSpec(slots.shape, lambda j: (0, 0))]
        + [pl.BlockSpec((block.shape[0], step), lambda j: (0, j)) for block in blocks],
        out_specs=pl.BlockSpec((rows, step), lambda j: (0, j)),
        compiler_params=params(),
        cost_estimate=cost(),
        name="gather_rows",
    )(slots, *blocks)


def along(array, group_bit, replica_bits):
    groups, replicas = lax.axis_size("group"), lax.axis_size("rep")
    pairs = [
        (g * replicas + r, (g ^ group_bit) * replicas + (r ^ replica_bits))
        for g in range(groups)
        for r in range(replicas)
    ]
    return lax.ppermute(array, ("group", "rep"), pairs)


def shared_local(
    queries,
    current_key_value,
    key_value_pool,
    request_page_entries,
    context_length,
    migration_page,
    migration_target,
    adapter_replica,
    adapter_position,
    adapter_down_weight,
    adapter_up_weight,
):
    rows, width = queries.shape
    replicas = lax.axis_size("rep")
    cap = 2 * rows // replicas
    group = lax.axis_index("group")
    half = group.reshape(1).astype(jnp.int32)
    where = jnp.stack([lax.axis_index("rep"), group]).astype(jnp.int32)
    targets = adapter_replica.reshape(1, -1)
    down_rows = jnp.swapaxes(adapter_down_weight, 1, 2)
    down = down_rows.reshape(-1, width)
    up = adapter_up_weight.reshape(-1, adapter_up_weight.shape[2])
    entries = request_page_entries.T
    lengths = context_length.reshape(1, -1)
    positions = adapter_position.reshape(1, -1)
    pages, page_len, features = key_value_pool.shape
    pool = key_value_pool.reshape(pages * page_len, features)

    columns = up.shape[1]
    early = columns // 8 * 5
    rank = up.shape[0] // 2
    outgoing, *packs = outgoing_pages(
        half,
        migration_page,
        migration_target,
        key_value_pool,
        replicas,
        (down_rows, adapter_up_weight),
        (((0, width, 0, 0),), ((0, early, 1, 0), (early, columns, 2, 0))),
        ((rank, width), (rank, early), (rank, columns - early)),
    )
    arrived = lax.all_to_all(outgoing, "rep", split_axis=0, concat_axis=0, tiled=True)
    found = attend_pool(queries, pool, entries, lengths, page_len)
    first = [along(*after(packs[:1], arrived, found[1]), 0, 6), along(packs[1], 0, 6)]

    def place(targets, replica):
        apart = jnp.bitwise_xor(targets, replica)
        far = jnp.right_shift(apart, 2)
        return (2 * jnp.bitwise_xor(jnp.bitwise_and(apart, 3), 2 * far) + far) * cap

    slots, here, *outbound = finish(
        where,
        queries,
        found,
        arrived.reshape(-1, features),
        current_key_value,
        entries,
        lengths,
        targets,
        positions,
        page_len,
        pages * page_len,
        (2 * cap,) * 4,
        place,
    )
    blocks = [along(block, 0, 3 - b) for b, block in enumerate(outbound[::-1])]
    blocks = [here] + blocks[::-1]
    first.append(along(*after([packs[2]], blocks[3]), 0, 6))
    second = [along(*after([first[0]], slots), 1, 0), along(*after([first[1]], blocks[1]), 1, 0)]
    mine = low_products(half, blocks, down, first[0], second[0])
    other = lax.ppermute(mine, "tp", [(0, 1), (1, 0)])
    second.append(along(*after([first[2]], other), 1, 0))
    own = lift_own(mine, other, up)
    own = [block if b == 0 else along(block, 0, b) for b, block in enumerate(own)]
    far = lift_far(half, mine, other, first[1:], second[1:])
    far = [block if b == 0 else along(block, 0, b) for b, block in enumerate(far)]
    return gather_rows(slots, [block for pair in zip(own, far) for block in pair])


def local(
    queries,
    current_key_value,
    key_value_pool,
    request_page_entries,
    context_length,
    migration_page,
    migration_target,
    adapter_replica,
    adapter_position,
    adapter_down_weight,
    adapter_up_weight,
):
    replicas = lax.axis_size("rep")
    if replicas == 8 and lax.axis_size("group") == 2 and adapter_down_weight.shape[0] == 2:
        return shared_local(
            queries,
            current_key_value,
            key_value_pool,
            request_page_entries,
            context_length,
            migration_page,
            migration_target,
            adapter_replica,
            adapter_position,
            adapter_down_weight,
            adapter_up_weight,
        )
    rows, width = queries.shape
    adapter_number = adapter_down_weight.shape[0]
    slot_cap = max(2, (2 * rows + replicas - 1) // replicas)
    entries = request_page_entries.T
    lengths = context_length.reshape(1, -1)
    pages, page_len, features = key_value_pool.shape
    pool = key_value_pool.reshape(pages * page_len, features)
    where = jnp.stack([lax.axis_index("rep"), lax.axis_index("group")]).astype(jnp.int32)
    (outgoing,) = outgoing_pages(where, migration_page, migration_target, key_value_pool, replicas)
    arrived = lax.all_to_all(outgoing, "rep", split_axis=0, concat_axis=0, tiled=True)
    found = attend_pool(queries, pool, entries, lengths, page_len)
    slots, outbound = finish(
        where,
        queries,
        found,
        arrived.reshape(-1, features),
        current_key_value,
        entries,
        lengths,
        adapter_replica.reshape(1, -1),
        adapter_position.reshape(1, -1),
        page_len,
        pages * page_len,
        (replicas * slot_cap,),
        lambda targets, replica: targets * slot_cap,
    )
    outbound = outbound.reshape(replicas, slot_cap, -1)
    activations = lax.all_to_all(outbound, "rep", split_axis=0, concat_axis=0, tiled=True)
    shape_in = activations.shape
    flat_output = activations.reshape(-1, shape_in[2])
    selector = (
        flat_output[:, width : width + 1].astype(jnp.int32)
        == jnp.arange(adapter_number, dtype=jnp.int32)[None, :]
    )
    reduced_rank_total = jnp.einsum(
        "oh,pht->opt", flat_output[:, :width], adapter_down_weight, preferred_element_type=jnp.float32
    )
    partial_low = jnp.sum(jnp.where(selector[:, :, None], reduced_rank_total, 0.0), axis=1)
    low_rank = lax.psum(partial_low, "tp").astype(jnp.bfloat16)
    broadcast_result = jnp.where(
        selector[:, :, None], low_rank[:, None, :], jnp.zeros((), jnp.bfloat16)
    )
    broadcast_result = broadcast_result.reshape(flat_output.shape[0], -1)
    lifted = jnp.dot(
        broadcast_result,
        adapter_up_weight.reshape(-1, adapter_up_weight.shape[2]),
        preferred_element_type=jnp.float32,
    )
    lifted = lifted.astype(jnp.bfloat16).reshape(shape_in[0], shape_in[1], -1)
    returned = lax.all_to_all(lifted, "rep", split_axis=0, concat_axis=0, tiled=True)
    route_mask = (
        jnp.arange(replicas * slot_cap, dtype=jnp.int32)[:, None] == slots
    ).astype(jnp.bfloat16)
    delta = jnp.einsum(
        "sr,sd->rd",
        route_mask,
        returned.reshape(replicas * slot_cap, -1),
        preferred_element_type=jnp.float32,
    )
    return delta.astype(jnp.bfloat16)


def solution(mesh):
    return jax.shard_map(
        local,
        mesh=mesh,
        in_specs=(
            P(("group", "rep"), "tp"),
            P(("group", "rep"), "tp"),
            P(("group", "rep"), None, "tp"),
            P(("group", "rep"), None),
            P(("group", "rep")),
            P(("group", "rep")),
            P(("group", "rep")),
            P(("group", "rep"), None),
            P(("group", "rep")),
            P("rep", "tp", None),
            P("rep", None, "tp"),
        ),
        out_specs=P(("group", "rep"), "tp"),
        check_vma=False,
    )
```

```python
import functools
import math

import jax
import jax.numpy as jnp
from jax import lax
from jax.experimental import pallas as pl
from jax.experimental.pallas import tpu as pltpu
from jax.sharding import PartitionSpec as P

HEAD_SIZE = 128
QUERY_GROUP = 8
MCAP = 2
LANES = 128
TOKEN_STEP = 256
HIDDEN = -1e30
SCORE_SCALE = math.log2(math.e) / math.sqrt(HEAD_SIZE)
BIAS_UNIT = float(jnp.bfloat16(1.0 / SCORE_SCALE))
HEADS_STEP = 2
MIB = 1024 * 1024


def whole(array):
    shape = array.shape
    return pl.BlockSpec(shape, lambda *step: (0,) * len(shape))


def smem_spec():
    return pl.BlockSpec(memory_space=pltpu.SMEM)


def params(mebibytes=24):
    return pltpu.CompilerParams(vmem_limit_bytes=mebibytes * MIB)


def cost():
    return pl.CostEstimate(flops=1024, bytes_accessed=1024, transcendentals=0)


def row_to_column(row):
    count = row.shape[1]
    across = lax.broadcasted_iota(jnp.int32, (count, count), 1)
    down = lax.broadcasted_iota(jnp.int32, (count, count), 0)
    return jnp.sum(jnp.where(across == down, row, 0), axis=1, keepdims=True)


def outgoing_kernel(pieces, half_ref, page_ref, target_ref, pool_ref, *refs):
    count_ref, chosen_ref, page_sem, share_sem = refs[-4:]
    out_ref, share_refs, mine_refs = refs[len(pieces)], refs[: len(pieces)], refs[len(pieces) + 1 : -4]
    entry_number = page_ref.shape[0]
    slot_number = out_ref.shape[0]

    def clear(slot, carry):
        chosen_ref[slot] = 0
        count_ref[slot // MCAP] = 0
        return carry

    def place(entry, carry):
        target = target_ref[entry]
        rank = count_ref[target]
        chosen_ref[target * MCAP + rank] = page_ref[entry]
        count_ref[target] = rank + 1
        return carry

    def page_copy(slot):
        return pltpu.make_async_copy(
            pool_ref.at[chosen_ref[slot]], out_ref.at[slot], page_sem.at[slot]
        )

    def send(slot, carry):
        page_copy(slot).start()
        return carry

    def finish(slot, carry):
        page_copy(slot).wait()
        return carry

    shares = []
    for share, cuts in zip(share_refs, pieces):
        for first, last, pack, start in cuts:
            shares.append(
                pltpu.make_async_copy(
                    share.at[half_ref[0], :, pl.ds(first, last - first)],
                    mine_refs[pack].at[:, pl.ds(start, last - first)],
                    share_sem.at[len(shares)],
                )
            )
    for share in shares:
        share.start()
    unroll = slot_number <= 16
    lax.fori_loop(0, slot_number, clear, 0, unroll=unroll)
    lax.fori_loop(0, entry_number, place, 0, unroll=unroll)
    lax.fori_loop(0, slot_number, send, 0, unroll=unroll)
    lax.fori_loop(0, slot_number, finish, 0, unroll=unroll)
    for share in shares:
        share.wait()


def outgoing_pages(half, migration_page, migration_target, pool, replicas, shares=(), pieces=(), packs=()):
    slots = replicas * MCAP
    hbm = pl.BlockSpec(memory_space=pltpu.HBM)
    out_shape = [jax.ShapeDtypeStruct((slots,) + pool.shape[1:], pool.dtype)]
    out_shape += [jax.ShapeDtypeStruct(pack, pool.dtype) for pack in packs]
    return pl.pallas_call(
        functools.partial(outgoing_kernel, pieces),
        out_shape=out_shape,
        in_specs=[smem_spec()] * 3 + [hbm] * (1 + len(shares)),
        out_specs=[whole(out) for out in out_shape],
        scratch_shapes=[
            pltpu.SMEM((replicas,), jnp.int32),
            pltpu.SMEM((slots,), jnp.int32),
            pltpu.SemaphoreType.DMA((slots,)),
            pltpu.SemaphoreType.DMA((max(1, sum(len(cuts) for cuts in pieces)),)),
        ],
        compiler_params=params(60),
        cost_estimate=cost(),
        name="outgoing_pages",
    )(half, migration_page, migration_target, pool, *shares)


def token_bias(entries, lengths, first_token, tokens, page_len):
    shape = (tokens, entries.shape[1])
    token = first_token + lax.broadcasted_iota(jnp.int32, shape, 0)
    seen = jnp.zeros(shape, jnp.float32)
    for e in range(entries.shape[0]):
        low = entries[e : e + 1, :] * page_len
        high = low + jnp.clip(lengths - e * page_len, 0, page_len)
        seen = seen + jnp.where((token >= low) & (token < high), 1.0, 0.0)
    return jnp.where(seen > 0.0, jnp.log2(jnp.maximum(seen, 1.0)), HIDDEN)


def identity(rows, on, off):
    across = lax.broadcasted_iota(jnp.int32, (rows, rows), 1)
    down = lax.broadcasted_iota(jnp.int32, (rows, rows), 0)
    return jnp.where(across == down, on, off)


def fill_queries(wide_query_ref, rows):
    ones = identity(rows, BIAS_UNIT, 0.0).astype(jnp.bfloat16)
    for h in range(wide_query_ref.shape[0] // rows):
        wide_query_ref[h * rows : (h + 1) * rows, HEAD_SIZE:] = ones


def fill_keys(wide_key_ref, entries_ref, length_ref, first_token, tokens, page_len):
    for start in range(0, tokens, TOKEN_STEP):
        size = min(TOKEN_STEP, tokens - start)
        bias = token_bias(entries_ref[...], length_ref[...], first_token + start, size, page_len)
        wide_key_ref[start : start + size, HEAD_SIZE:] = bias.astype(jnp.bfloat16)


def score_block(block, wide_query_ref, wide_key_ref, score_ref):
    tokens = score_ref.shape[1]
    top = None
    for start in range(0, tokens, TOKEN_STEP):
        size = min(TOKEN_STEP, tokens - start)
        part = lax.dot_general(
            wide_query_ref[block, :],
            wide_key_ref[start : start + size, :],
            (((1,), (1,)), ((), ())),
            preferred_element_type=jnp.float32,
        )
        score_ref[block, start : start + size] = part
        for lane in range(0, size, LANES):
            piece = part[:, lane : lane + LANES]
            top = piece if top is None else jnp.maximum(top, piece)
    return jnp.max(top, axis=1, keepdims=True)


def weigh_block(block, top, score_ref, weight_ref, wide_value_ref):
    tokens = score_ref.shape[1]
    for start in range(0, tokens, TOKEN_STEP):
        size = min(TOKEN_STEP, tokens - start)
        weights = jnp.exp2((score_ref[block, start : start + size] - top) * SCORE_SCALE)
        weight_ref[block, start : start + size] = weights.astype(jnp.bfloat16)
    return jnp.dot(weight_ref[block, :], wide_value_ref[...], preferred_element_type=jnp.float32)


def load_heads(wide_query_ref, query_ref):
    rows = query_ref.shape[0]
    for h in range(QUERY_GROUP):
        wide_query_ref[h * rows : (h + 1) * rows, :HEAD_SIZE] = query_ref[
            :, h * HEAD_SIZE : (h + 1) * HEAD_SIZE
        ]


def pool_kernel(page_len, query_ref, pool_ref, entries_ref, length_ref, part_ref, stat_ref, *refs):
    wide_query_ref, wide_key_ref, wide_value_ref, score_ref, weight_ref = refs
    rows = query_ref.shape[0]
    tokens = pool_ref.shape[0]

    @pl.when(pl.program_id(0) == 0)
    def _():
        fill_queries(wide_query_ref, rows)
        fill_keys(wide_key_ref, entries_ref, length_ref, 0, tokens, page_len)
        wide_value_ref[:, HEAD_SIZE:] = jnp.ones((tokens, HEAD_SIZE), jnp.bfloat16)

    wide_key_ref[:, :HEAD_SIZE] = pool_ref[:, :HEAD_SIZE]
    wide_value_ref[:, :HEAD_SIZE] = pool_ref[:, HEAD_SIZE:]
    load_heads(wide_query_ref, query_ref)
    lane = lax.broadcasted_iota(jnp.int32, (rows, LANES), 1)
    stats = jnp.zeros((rows, LANES), jnp.float32)
    for h in range(0, QUERY_GROUP, HEADS_STEP):
        block = slice(h * rows, (h + HEADS_STEP) * rows)
        top = score_block(block, wide_query_ref, wide_key_ref, score_ref)
        parts = weigh_block(block, top, score_ref, weight_ref, wide_value_ref)
        total = parts[:, HEAD_SIZE:]
        part_ref[block, :] = (parts[:, :HEAD_SIZE] / total).astype(jnp.bfloat16)
        level = top + jnp.log2(total) * (1.0 / SCORE_SCALE)
        for step in range(HEADS_STEP):
            own = slice(step * rows, (step + 1) * rows)
            stats = jnp.where(lane == h + step, level[own], stats)
    stat_ref[...] = stats


def attend_pool(queries, pool, entries, lengths, page_len):
    rows, width = queries.shape
    tokens = pool.shape[0]
    kv_local = pool.shape[1] // (2 * HEAD_SIZE)
    stacked = QUERY_GROUP * rows
    return pl.pallas_call(
        functools.partial(pool_kernel, page_len),
        grid=(kv_local,),
        out_shape=[
            jax.ShapeDtypeStruct((kv_local * stacked, LANES), jnp.bfloat16),
            jax.ShapeDtypeStruct((rows, kv_local * LANES), jnp.float32),
        ],
        in_specs=[
            pl.BlockSpec((rows, width // kv_local), lambda g: (0, g)),
            pl.BlockSpec((tokens, 2 * HEAD_SIZE), lambda g: (0, g)),
            whole(entries),
            whole(lengths),
        ],
        out_specs=[
            pl.BlockSpec((stacked, LANES), lambda g: (g, 0)),
            pl.BlockSpec((rows, LANES), lambda g: (0, g)),
        ],
        scratch_shapes=[
            pltpu.VMEM((stacked, 2 * HEAD_SIZE), jnp.bfloat16),
            pltpu.VMEM((tokens, 2 * HEAD_SIZE), jnp.bfloat16),
            pltpu.VMEM((tokens, 2 * HEAD_SIZE), jnp.bfloat16),
            pltpu.VMEM((stacked, tokens), jnp.float32),
            pltpu.VMEM((stacked, tokens), jnp.bfloat16),
        ],
        compiler_params=params(),
        cost_estimate=pl.CostEstimate(10**9, 10**7, 10**6),
        name="attend_pool",
    )(queries, pool, entries, lengths)


def finish_kernel(
    page_len,
    first_token,
    place,
    where_ref,
    query_ref,
    part_ref,
    stat_ref,
    arrived_ref,
    fresh_ref,
    entries_ref,
    length_ref,
    target_ref,
    position_ref,
    slot_ref,
    *refs,
):
    out_refs, refs = refs[:-6], refs[-6:]
    wide_query_ref, wide_key_ref, wide_value_ref, score_ref, weight_ref, heads_ref = refs
    rows = query_ref.shape[0]
    g = pl.program_id(0)
    tokens = arrived_ref.shape[0]

    @pl.when(g == 0)
    def _():
        fill_queries(wide_query_ref, rows)
        fill_keys(wide_key_ref, entries_ref, length_ref, first_token, tokens, page_len)
        wide_key_ref[tokens:, HEAD_SIZE:] = identity(rows, 0.0, HIDDEN).astype(jnp.bfloat16)
        wide_value_ref[:, HEAD_SIZE:] = jnp.ones((tokens + rows, HEAD_SIZE), jnp.bfloat16)

    for shelf, first in ((arrived_ref, 0), (fresh_ref, tokens)):
        own = slice(first, first + shelf.shape[0])
        wide_key_ref[own, :HEAD_SIZE] = shelf[:, :HEAD_SIZE]
        wide_value_ref[own, :HEAD_SIZE] = shelf[:, HEAD_SIZE:]
    load_heads(wide_query_ref, query_ref)
    for h in range(0, QUERY_GROUP, HEADS_STEP):
        block = slice(h * rows, (h + HEADS_STEP) * rows)
        level = jnp.concatenate(
            [stat_ref[:, h + step : h + step + 1] for step in range(HEADS_STEP)], axis=0
        )
        top = jnp.maximum(score_block(block, wide_query_ref, wide_key_ref, score_ref), level)
        parts = weigh_block(block, top, score_ref, weight_ref, wide_value_ref)
        pool_weight = jnp.exp2((level - top) * SCORE_SCALE)
        heads = parts[:, :HEAD_SIZE] + pool_weight * part_ref[block, :].astype(jnp.float32)
        heads = (heads / (parts[:, HEAD_SIZE:] + pool_weight)).astype(jnp.bfloat16)
        for step in range(HEADS_STEP):
            heads_ref[g, :, (h + step) * HEAD_SIZE : (h + step + 1) * HEAD_SIZE] = heads[
                step * rows : (step + 1) * rows
            ]

    @pl.when(g == pl.num_programs(0) - 1)
    def _():
        targets = target_ref[...]
        across = lax.broadcasted_iota(jnp.int32, (rows, rows), 1)
        down = lax.broadcasted_iota(jnp.int32, (rows, rows), 0)
        earlier = (row_to_column(targets) == targets) & (down < across)
        rank = jnp.sum(earlier.astype(jnp.int32), axis=0, keepdims=True)
        slots_of = place(targets, where_ref[0]) + rank
        slot_ref[...] = slots_of
        wide = heads_ref.shape[2]
        first = 0
        for out_ref in out_refs:
            slots = out_ref.shape[0]
            slot = first + lax.broadcasted_iota(jnp.int32, (slots, rows), 0)
            pick = slot == slots_of
            label = jnp.sum(jnp.where(pick, position_ref[...], 0), axis=1, keepdims=True)
            pick = pick.astype(jnp.float32).astype(jnp.bfloat16)
            for kv in range(heads_ref.shape[0]):
                out_ref[:, kv * wide : (kv + 1) * wide] = jnp.dot(
                    pick, heads_ref[kv], preferred_element_type=jnp.float32
                ).astype(jnp.bfloat16)
            out_ref[:, heads_ref.shape[0] * wide :] = jnp.broadcast_to(
                label.astype(jnp.float32).astype(jnp.bfloat16), (slots, LANES)
            )
            first += slots


def finish(
    where, queries, found, arrived, fresh, entries, lengths, targets, positions, page_len, first_token, blocks, place
):
    rows, width = queries.shape
    kv_local = arrived.shape[1] // (2 * HEAD_SIZE)
    tokens = arrived.shape[0] + rows
    stacked = QUERY_GROUP * rows
    shelf = lambda array: pl.BlockSpec((array.shape[0], 2 * HEAD_SIZE), lambda g: (0, g))
    small = (entries, lengths, targets, positions)
    out_shape = [jax.ShapeDtypeStruct((1, rows), jnp.int32)]
    out_shape += [jax.ShapeDtypeStruct((block, width + LANES), jnp.bfloat16) for block in blocks]
    return pl.pallas_call(
        functools.partial(finish_kernel, page_len, first_token, place),
        grid=(kv_local,),
        out_shape=out_shape,
        in_specs=[
            smem_spec(),
            pl.BlockSpec((rows, width // kv_local), lambda g: (0, g)),
            pl.BlockSpec((stacked, LANES), lambda g: (g, 0)),
            pl.BlockSpec((rows, LANES), lambda g: (0, g)),
        ]
        + [shelf(array) for array in (arrived, fresh)]
        + [whole(array) for array in small],
        out_specs=[whole(block) for block in out_shape],
        scratch_shapes=[
            pltpu.VMEM((stacked, 2 * HEAD_SIZE), jnp.bfloat16),
            pltpu.VMEM((tokens, 2 * HEAD_SIZE), jnp.bfloat16),
            pltpu.VMEM((tokens, 2 * HEAD_SIZE), jnp.bfloat16),
            pltpu.VMEM((stacked, tokens), jnp.float32),
            pltpu.VMEM((stacked, tokens), jnp.bfloat16),
            pltpu.VMEM((kv_local, rows, width // kv_local), jnp.bfloat16),
        ],
        compiler_params=params(12 + tokens * stacked * 7 // MIB),
        cost_estimate=cost(),
        name="finish",
    )(where, queries, *found, arrived, fresh, *small)


def after_kernel(*refs):
    pass


def after(arrays, *others):
    hbm = pl.BlockSpec(memory_space=pl.ANY)
    return pl.pallas_call(
        after_kernel,
        out_shape=[jax.ShapeDtypeStruct(array.shape, array.dtype) for array in arrays],
        in_specs=[hbm] * (len(arrays) + len(others)),
        out_specs=[hbm] * len(arrays),
        input_output_aliases={i: i for i in range(len(arrays))},
        compiler_params=params(1),
        cost_estimate=cost(),
        name="after",
    )(*arrays, *others)


def down_kernel(half_ref, *refs):
    block_refs, (own_ref, first_ref, second_ref, out_ref, rows_ref) = refs[:-5], refs[-5:]
    cap = out_ref.shape[0] // 8
    width = own_ref.shape[1]
    for b, block in enumerate(block_refs):
        rows_ref[b * cap : (b + 1) * cap, :] = block[:cap, :]
        rows_ref[(b + 4) * cap : (b + 5) * cap, :] = block[cap:, :]
    swapped = half_ref[0] == 1
    zero = jnp.where(swapped, second_ref[...], first_ref[...])
    one = jnp.where(swapped, first_ref[...], second_ref[...])
    lane = lax.broadcasted_iota(jnp.int32, (1, out_ref.shape[1]), 1)
    adapter = jnp.where(lane < out_ref.shape[1] // 2, 0.0, 1.0)
    for start, weights in ((0, own_ref[...]), (4 * cap, jnp.concatenate([zero, one], axis=0))):
        part = slice(start, start + 4 * cap)
        product = lax.dot_general(
            rows_ref[part, :width],
            weights,
            (((1,), (1,)), ((), ())),
            preferred_element_type=jnp.float32,
        )
        label = rows_ref[part, width:].astype(jnp.float32)
        out_ref[part, :] = jnp.where(label == adapter, product, 0.0)


def low_products(half, blocks, own, first, second):
    rows = sum(block.shape[0] for block in blocks)
    inputs = (*blocks, own, first, second)
    out_shape = jax.ShapeDtypeStruct((rows, own.shape[0]), jnp.float32)
    return pl.pallas_call(
        down_kernel,
        grid=(1,),
        out_shape=out_shape,
        in_specs=[smem_spec()]
        + [whole(array) for array in (*blocks, own)]
        + [pl.BlockSpec((first.shape[0], own.shape[1]), lambda *step: (0, 0))] * 2,
        out_specs=whole(out_shape),
        scratch_shapes=[pltpu.VMEM((rows, blocks[0].shape[1]), jnp.bfloat16)],
        compiler_params=params(),
        cost_estimate=cost(),
        name="low_products",
    )(half, *inputs)


def lift(low_refs, weights, out_refs):
    low = (low_refs[0][...] + low_refs[1][...]).astype(jnp.bfloat16)
    lifted = jnp.dot(low, weights, preferred_element_type=jnp.float32).astype(jnp.bfloat16)
    cap = out_refs[0].shape[0]
    for b, out_ref in enumerate(out_refs):
        out_ref[...] = lifted[b * cap : (b + 1) * cap]


def lift_own_kernel(mine_ref, other_ref, own_ref, *out_refs):
    lift((mine_ref, other_ref), own_ref[...], out_refs)


def lift_own(mine, other, weights):
    rows, rank = mine.shape
    width = weights.shape[1]
    step = width
    low = pl.BlockSpec((rows // 2, rank), lambda j: (0, 0))
    out = jax.ShapeDtypeStruct((rows // 8, width), jnp.bfloat16)
    return pl.pallas_call(
        lift_own_kernel,
        grid=(width // step,),
        out_shape=(out,) * 4,
        in_specs=[low, low, pl.BlockSpec((rank, step), lambda j: (0, j))],
        out_specs=[pl.BlockSpec((rows // 8, step), lambda j: (0, j))] * 4,
        compiler_params=params(),
        cost_estimate=cost(),
        name="lift_own",
    )(mine, other, weights)


def lift_far_kernel(half_ref, mine_ref, other_ref, *refs):
    number = (len(refs) - 4) // 2
    first_refs, second_refs, out_refs = refs[:number], refs[number : 2 * number], refs[2 * number :]
    low = (mine_ref[...] + other_ref[...]).astype(jnp.bfloat16)
    swapped = half_ref[0] == 1
    cap = out_refs[0].shape[0]
    place = 0
    for first_ref, second_ref in zip(first_refs, second_refs):
        columns = slice(place, place + first_ref.shape[1])
        zero = jnp.where(swapped, second_ref[...], first_ref[...])
        one = jnp.where(swapped, first_ref[...], second_ref[...])
        lifted = jnp.dot(
            low, jnp.concatenate([zero, one], axis=0), preferred_element_type=jnp.float32
        ).astype(jnp.bfloat16)
        for b, out_ref in enumerate(out_refs):
            out_ref[:, columns] = lifted[b * cap : (b + 1) * cap]
        place = columns.stop


def lift_far(half, mine, other, first, second):
    rows, rank = mine.shape
    width = sum(piece.shape[1] for piece in first)
    low = pl.BlockSpec((rows // 2, rank), lambda j: (1, 0))
    out = jax.ShapeDtypeStruct((rows // 8, width), jnp.bfloat16)
    return pl.pallas_call(
        lift_far_kernel,
        grid=(1,),
        out_shape=(out,) * 4,
        in_specs=[smem_spec(), low, low] + [whole(piece) for piece in (*first, *second)],
        out_specs=[whole(out)] * 4,
        compiler_params=params(),
        cost_estimate=cost(),
        name="lift_far",
    )(half, mine, other, *first, *second)


def gather_rows_kernel(slot_ref, *refs):
    out_ref = refs[-1]
    rows = out_ref.shape[0]
    stacked = jnp.concatenate([ref[...] for ref in refs[:-1]], axis=0)
    slot = lax.broadcasted_iota(jnp.int32, (rows, stacked.shape[0]), 1)
    pick = (slot == row_to_column(slot_ref[...])).astype(jnp.float32).astype(jnp.bfloat16)
    out_ref[...] = jnp.dot(pick, stacked, preferred_element_type=jnp.float32).astype(jnp.bfloat16)


def gather_rows(slots, blocks):
    rows = slots.shape[1]
    width = blocks[0].shape[1]
    step = 4096
    return pl.pallas_call(
        gather_rows_kernel,
        grid=(width // step,),
        out_shape=jax.ShapeDtypeStruct((rows, width), jnp.bfloat16),
        in_specs=[pl.BlockSpec(slots.shape, lambda j: (0, 0))]
        + [pl.BlockSpec((block.shape[0], step), lambda j: (0, j)) for block in blocks],
        out_specs=pl.BlockSpec((rows, step), lambda j: (0, j)),
        compiler_params=params(),
        cost_estimate=cost(),
        name="gather_rows",
    )(slots, *blocks)


def along(array, group_bit, replica_bits):
    groups, replicas = lax.axis_size("group"), lax.axis_size("rep")
    pairs = [
        (g * replicas + r, (g ^ group_bit) * replicas + (r ^ replica_bits))
        for g in range(groups)
        for r in range(replicas)
    ]
    return lax.ppermute(array, ("group", "rep"), pairs)


def shared_local(
    queries,
    current_key_value,
    key_value_pool,
    request_page_entries,
    context_length,
    migration_page,
    migration_target,
    adapter_replica,
    adapter_position,
    adapter_down_weight,
    adapter_up_weight,
):
    rows, width = queries.shape
    replicas = lax.axis_size("rep")
    cap = 2 * rows // replicas
    group = lax.axis_index("group")
    half = group.reshape(1).astype(jnp.int32)
    where = jnp.stack([lax.axis_index("rep"), group]).astype(jnp.int32)
    targets = adapter_replica.reshape(1, -1)
    down_rows = jnp.swapaxes(adapter_down_weight, 1, 2)
    down = down_rows.reshape(-1, width)
    up = adapter_up_weight.reshape(-1, adapter_up_weight.shape[2])
    entries = request_page_entries.T
    lengths = context_length.reshape(1, -1)
    positions = adapter_position.reshape(1, -1)
    pages, page_len, features = key_value_pool.shape
    pool = key_value_pool.reshape(pages * page_len, features)

    columns = up.shape[1]
    early = columns // 8 * 5
    rank = up.shape[0] // 2
    outgoing, *packs = outgoing_pages(
        half,
        migration_page,
        migration_target,
        key_value_pool,
        replicas,
        (down_rows, adapter_up_weight),
        (((0, width, 0, 0),), ((0, early, 1, 0), (early, columns, 2, 0))),
        ((rank, width), (rank, early), (rank, columns - early)),
    )
    arrived = lax.all_to_all(outgoing, "rep", split_axis=0, concat_axis=0, tiled=True)
    found = attend_pool(queries, pool, entries, lengths, page_len)
    first = [along(*after(packs[:1], arrived, found[1]), 0, 6), along(packs[1], 0, 6)]

    def place(targets, replica):
        apart = jnp.bitwise_xor(targets, replica)
        far = jnp.right_shift(apart, 2)
        return (2 * jnp.bitwise_xor(jnp.bitwise_and(apart, 3), 2 * far) + far) * cap

    slots, here, *outbound = finish(
        where,
        queries,
        found,
        arrived.reshape(-1, features),
        current_key_value,
        entries,
        lengths,
        targets,
        positions,
        page_len,
        pages * page_len,
        (2 * cap,) * 4,
        place,
    )
    blocks = [along(block, 0, 3 - b) for b, block in enumerate(outbound[::-1])]
    blocks = [here] + blocks[::-1]
    first.append(along(*after([packs[2]], blocks[3]), 0, 6))
    second = [along(*after([first[0]], slots), 1, 0), along(*after([first[1]], blocks[1]), 1, 0)]
    mine = low_products(half, blocks, down, first[0], second[0])
    other = lax.ppermute(mine, "tp", [(0, 1), (1, 0)])
    second.append(along(*after([first[2]], other), 1, 0))
    own = lift_own(mine, other, up)
    own = [own[0], *[along(own[b], 0, b) for b in (3, 2, 1)][::-1]]
    far = lift_far(half, mine, other, first[1:], second[1:])
    far = [far[0], *[along(far[b], 0, b) for b in (3, 2, 1)][::-1]]
    return gather_rows(slots, [block for pair in zip(own, far) for block in pair])


def local(
    queries,
    current_key_value,
    key_value_pool,
    request_page_entries,
    context_length,
    migration_page,
    migration_target,
    adapter_replica,
    adapter_position,
    adapter_down_weight,
    adapter_up_weight,
):
    replicas = lax.axis_size("rep")
    if replicas == 8 and lax.axis_size("group") == 2 and adapter_down_weight.shape[0] == 2:
        return shared_local(
            queries,
            current_key_value,
            key_value_pool,
            request_page_entries,
            context_length,
            migration_page,
            migration_target,
            adapter_replica,
            adapter_position,
            adapter_down_weight,
            adapter_up_weight,
        )
    rows, width = queries.shape
    adapter_number = adapter_down_weight.shape[0]
    slot_cap = max(2, (2 * rows + replicas - 1) // replicas)
    entries = request_page_entries.T
    lengths = context_length.reshape(1, -1)
    pages, page_len, features = key_value_pool.shape
    pool = key_value_pool.reshape(pages * page_len, features)
    where = jnp.stack([lax.axis_index("rep"), lax.axis_index("group")]).astype(jnp.int32)
    (outgoing,) = outgoing_pages(where, migration_page, migration_target, key_value_pool, replicas)
    arrived = lax.all_to_all(outgoing, "rep", split_axis=0, concat_axis=0, tiled=True)
    found = attend_pool(queries, pool, entries, lengths, page_len)
    slots, outbound = finish(
        where,
        queries,
        found,
        arrived.reshape(-1, features),
        current_key_value,
        entries,
        lengths,
        adapter_replica.reshape(1, -1),
        adapter_position.reshape(1, -1),
        page_len,
        pages * page_len,
        (replicas * slot_cap,),
        lambda targets, replica: targets * slot_cap,
    )
    outbound = outbound.reshape(replicas, slot_cap, -1)
    activations = lax.all_to_all(outbound, "rep", split_axis=0, concat_axis=0, tiled=True)
    shape_in = activations.shape
    flat_output = activations.reshape(-1, shape_in[2])
    selector = (
        flat_output[:, width : width + 1].astype(jnp.int32)
        == jnp.arange(adapter_number, dtype=jnp.int32)[None, :]
    )
    reduced_rank_total = jnp.einsum(
        "oh,pht->opt", flat_output[:, :width], adapter_down_weight, preferred_element_type=jnp.float32
    )
    partial_low = jnp.sum(jnp.where(selector[:, :, None], reduced_rank_total, 0.0), axis=1)
    low_rank = lax.psum(partial_low, "tp").astype(jnp.bfloat16)
    broadcast_result = jnp.where(
        selector[:, :, None], low_rank[:, None, :], jnp.zeros((), jnp.bfloat16)
    )
    broadcast_result = broadcast_result.reshape(flat_output.shape[0], -1)
    lifted = jnp.dot(
        broadcast_result,
        adapter_up_weight.reshape(-1, adapter_up_weight.shape[2]),
        preferred_element_type=jnp.float32,
    )
    lifted = lifted.astype(jnp.bfloat16).reshape(shape_in[0], shape_in[1], -1)
    returned = lax.all_to_all(lifted, "rep", split_axis=0, concat_axis=0, tiled=True)
    route_mask = (
        jnp.arange(replicas * slot_cap, dtype=jnp.int32)[:, None] == slots
    ).astype(jnp.bfloat16)
    delta = jnp.einsum(
        "sr,sd->rd",
        route_mask,
        returned.reshape(replicas * slot_cap, -1),
        preferred_element_type=jnp.float32,
    )
    return delta.astype(jnp.bfloat16)


def solution(mesh):
    return jax.shard_map(
        local,
        mesh=mesh,
        in_specs=(
            P(("group", "rep"), "tp"),
            P(("group", "rep"), "tp"),
            P(("group", "rep"), None, "tp"),
            P(("group", "rep"), None),
            P(("group", "rep")),
            P(("group", "rep")),
            P(("group", "rep")),
            P(("group", "rep"), None),
            P(("group", "rep")),
            P("rep", "tp", None),
            P("rep", None, "tp"),
        ),
        out_specs=P(("group", "rep"), "tp"),
        check_vma=False,
    )
```
